32 devices in a mesh: region: 16 (over z, y, x), blk: 2 (over core).
Axes of the slice: x: 2, y: 2, z: 4, core: 2. Of those that a mesh axis runs over, the one named last changes fastest.
Arguments:
- site_tensors: float32 [128, 2, 32, 1024], P('region', 'blk'), may hold values from -18 to 18
- projectors: bfloat16 [128, 2, 32, 1024], P('region'), may hold values from -0.1875 to 0.1875
- gate_matrix: float32 [2, 2, 2, 2], replicated, may hold values from -3 to 3
- recv_src: int32 [128, 3], P('region'), may hold values from 0 to 88, as said below
- cut_list: int32 [160], P('region'), may hold values from 0 to 23, as said below
- cut_dest: int32 [16, 10], replicated, may hold values from -1 to 63, as said below
- gate_src: int32 [128], P('region'), may hold values from 0 to 24, as said below
- gate_list: int32 [32], P('region'), may hold values from 0 to 7, as said below
- gate_dest: int32 [16, 2], replicated, may hold values from -1 to 15, as said below
Outputs:
- new_sites: float32 [128, 2, 32, 1024], P('region', 'blk')
- messages: float32 [128, 3, 1024], P('region')
The draws below stay inside these ranges and needn't reach their ends.
Inputs may be any that keep to these rules, and one draw needn't show every extreme that they name: `recv_src`: messages between one ordered pair of regions use distinct slots below 4; some pair uses all 4. `cut_list`: entries whose cut_dest is -1 are padding. `cut_dest`: some region fills all 10 entries of its row. `gate_src`: gate partners form pairs along vertical links. `gate_list`: entries whose gate_dest is -1 are padding. `gate_dest`: some region fills all 2 entries of its row.
All inputs are finite; a program needn't handle non-finite values.
Results may differ from the reference program's by a relative error of at most 0.0039.
Values may be sent and summed in bfloat16 or wider, within the bound.
A program may use at most 128 MiB of HBM per device.

```python
import math
import jax
import jax.numpy as jnp
from jax import lax

D = 32
SITES_DEV = 8
SWEEPS = 2
CAP = 4
NSITES = 128
GCAP = 1
CUT_MAX = 10
GCUT = 2
N_REGION = 16


SQRT_THREE = math.sqrt(3.0)


def log_scale(key, shape, low_end, high_end):
    drawn = jnp.exp(jax.random.uniform(key, shape, jnp.float32, math.log(low_end), math.log(high_end)))
    average = (high_end - low_end) / math.log(high_end)
    return jnp.sqrt(drawn / average)


def draw_site_tensors(key, part):
    subkeys = jax.random.split(jax.random.fold_in(key, 11), 6)
    full_shape = (NSITES, 2, D, D, D)
    carry_shape = (NSITES, 2, 1, D, D)
    mixing_shape = (NSITES, 1, D, D, 1)
    rough_noise = jnp.clip(jax.random.normal(subkeys[0], full_shape, jnp.float32), -4.0, 4.0)
    carried_rows = SQRT_THREE * jnp.clip(jax.random.normal(subkeys[1], carry_shape, jnp.float32), -4.0, 4.0)
    mixing_noise = jnp.clip(jax.random.normal(subkeys[2], mixing_shape, jnp.float32), -4.0, 4.0)
    high_end = 10.0
    scale_left = log_scale(subkeys[3], (NSITES, 1, D, 1, 1), 1.0, high_end)
    scale_right = log_scale(subkeys[4], (NSITES, 1, 1, D, 1), 1.0, high_end)
    scale_vertical = log_scale(subkeys[5], (NSITES, 1, 1, 1, D), 1.0, high_end)
    rough_part = rough_noise * scale_left * scale_right * scale_vertical / math.sqrt(D)
    counter = jnp.arange(D, dtype=jnp.int32)
    diagonal = (counter[:, None] == counter[None, :]).astype(jnp.float32).reshape(1, 1, D, D, 1)
    mixing = diagonal + 0.5 * mixing_noise / math.sqrt(D)
    carried = mixing * carried_rows
    return (carried + rough_part).reshape(NSITES, 2, D, D * D)


def grid_columns(regions):
    columns = 1
    while columns * columns < regions or regions % columns != 0:
        columns += 1
    return columns


def lattice(key):
    per_dev = SITES_DEV
    regions = N_REGION
    tile_width = per_dev // 4
    bridges = (tile_width + 3) // 4
    tile_cols = grid_columns(regions)
    tile_rows = regions // tile_cols
    rows_all = 4 * tile_rows
    cols_all = tile_width * tile_cols
    base_key = jax.random.fold_in(key, 7)
    key_tiles, key_cells = jax.random.split(base_key)
    tile_device = jax.random.permutation(key_tiles, regions).astype(jnp.int32)
    cell_keys = jax.random.split(key_cells, regions)
    cell_local = jax.vmap(lambda single: jax.random.permutation(single, per_dev))(cell_keys).astype(jnp.int32)
    row_ids = jnp.broadcast_to(jnp.arange(rows_all, dtype=jnp.int32)[:, None], (rows_all, cols_all)).reshape(-1)
    col_ids = jnp.broadcast_to(jnp.arange(cols_all, dtype=jnp.int32)[None, :], (rows_all, cols_all)).reshape(-1)

    def locate(row_at, col_at):
        tile_id = row_at // 4 * tile_cols + col_at // tile_width
        cell_id = row_at % 4 * tile_width + col_at % tile_width
        return (tile_id, tile_device[tile_id], cell_local[tile_id, cell_id])
    tile_id, device, local_id = locate(row_ids, col_ids)
    downward = ((col_ids + 2 * (row_ids % 2)) % 4 == 0) & (row_ids < rows_all - 1)
    upward = ((col_ids + 2 * ((row_ids + 1) % 2)) % 4 == 0) & (row_ids > 0)
    near_rows = [row_ids, row_ids, jnp.where(downward, row_ids + 1, row_ids - 1)]
    near_cols = [col_ids - 1, col_ids + 1, col_ids]
    exists = [col_ids > 0, col_ids < cols_all - 1, downward | upward]
    back_leg = [1, 0, 2]
    link_pos = [row_ids % 4, row_ids % 4, col_ids % tile_width // 4]
    vertical_pos = jnp.where(upward, 0, bridges) + col_ids % tile_width // 4
    out_pos = [row_ids % 4, 4 + row_ids % 4, 8 + vertical_pos]
    msg_none = 3 * per_dev + regions * CAP
    gate_none = per_dev + regions * GCAP
    site_id = device * per_dev + local_id
    receive = jnp.zeros((regions * per_dev, 3), jnp.int32)
    send_list = jnp.zeros((regions * CUT_MAX,), jnp.int32)
    send_dest = jnp.full((regions * CUT_MAX,), -1, jnp.int32)
    gate_source = jnp.full((regions * per_dev,), gate_none, jnp.int32)
    gate_sites = jnp.zeros((regions * GCUT,), jnp.int32)
    gate_target = jnp.full((regions * GCUT,), -1, jnp.int32)
    for leg_index in range(3):
        near_row = jnp.clip(near_rows[leg_index], 0, rows_all - 1)
        near_col = jnp.clip(near_cols[leg_index], 0, cols_all - 1)
        near_tile, near_device, near_local = locate(near_row, near_col)
        inside = near_tile == tile_id
        crossing = exists[leg_index] & ~inside
        remote_value = 3 * per_dev + near_device * CAP + link_pos[leg_index]
        source_value = jnp.where(exists[leg_index], jnp.where(inside, 3 * near_local + back_leg[leg_index], remote_value), msg_none)
        receive = receive.at[site_id, leg_index].set(source_value.astype(jnp.int32))
        out_slot = jnp.where(crossing, device * CUT_MAX + out_pos[leg_index], regions * CUT_MAX)
        send_list = send_list.at[out_slot].set((3 * local_id + leg_index).astype(jnp.int32), mode='drop')
        send_dest = send_dest.at[out_slot].set((near_device * CAP + link_pos[leg_index]).astype(jnp.int32), mode='drop')
        if leg_index == 2:
            gate_value = jnp.where(exists[2], jnp.where(inside, near_local, per_dev + near_device * GCAP + link_pos[2]), gate_none)
            gate_source = gate_source.at[site_id].set(gate_value.astype(jnp.int32))
            gate_slot = jnp.where(crossing, device * GCUT + vertical_pos, regions * GCUT)
            gate_sites = gate_sites.at[gate_slot].set(local_id.astype(jnp.int32), mode='drop')
            gate_target = gate_target.at[gate_slot].set((near_device * GCAP + link_pos[2]).astype(jnp.int32), mode='drop')
    return (receive, send_list, send_dest.reshape(regions, CUT_MAX), gate_source, gate_sites, gate_target.reshape(regions, GCUT))


def draw_recv_src(key, part):
    return lattice(key)[0]


def draw_cut_list(key, part):
    return lattice(key)[1]


def draw_cut_dest(key, part):
    return lattice(key)[2]


def draw_gate_src(key, part):
    return lattice(key)[3]


def draw_gate_list(key, part):
    return lattice(key)[4]


def draw_gate_dest(key, part):
    return lattice(key)[5]


def block_scale(stream_key, extent, shards, smallest, high):
    def one(axis_at, blocks):
        heights = jax.random.uniform(jax.random.fold_in(jax.random.fold_in(stream_key, 6), axis_at), (blocks,), jnp.float32, smallest / len(shards), high / len(shards))
        return jnp.repeat(jnp.exp(heights), extent[axis_at] // blocks).reshape((-1,) + (1,) * (len(extent) - axis_at - 1))

    level = one(*shards[0])
    for cut in shards[1:]:
        level = level * one(*cut)
    return level


def gaussian(stream_key, extent, spread, reach, cuts=(), held_as=jnp.bfloat16):
    values = jax.random.normal(stream_key, extent, jnp.float32) * spread
    if len(cuts) > 0:
        values = block_scale(stream_key, extent, cuts, -0.22, 0.18) * values
    return jnp.clip(values, min=-reach, max=reach).astype(held_as)


def setup_inputs(seed: int = 0) -> dict:
    key_of = jax.random.split(jax.random.key(seed), 10)
    site_tensors = draw_site_tensors(jax.random.fold_in(key_of[9], 71), 0)
    projectors = gaussian(key_of[1], (NSITES, 2, D, D * D), (D * D) ** -0.5, 0.1875, ((0, 16),))
    gate_matrix = gaussian(key_of[2], (2, 2, 2, 2), 4 ** -0.5, 3.0, (), jnp.float32)
    recv_src = draw_recv_src(jax.random.fold_in(key_of[9], 71), 0)
    cut_list = draw_cut_list(jax.random.fold_in(key_of[9], 71), 0)
    cut_dest = draw_cut_dest(jax.random.fold_in(key_of[9], 71), 0)
    gate_src = draw_gate_src(jax.random.fold_in(key_of[9], 71), 0)
    gate_list = draw_gate_list(jax.random.fold_in(key_of[9], 71), 0)
    gate_dest = draw_gate_dest(jax.random.fold_in(key_of[9], 71), 0)
    return dict(site_tensors=site_tensors, projectors=projectors, gate_matrix=gate_matrix, recv_src=recv_src, cut_list=cut_list, cut_dest=cut_dest, gate_src=gate_src, gate_list=gate_list, gate_dest=gate_dest)


HIGHEST = lax.Precision.HIGHEST
EPSILON = 1e-06

def weighted(tensors, incoming):
    partial_a = jnp.einsum('isabc,iag->isgbc', tensors, incoming[:, 0], precision=HIGHEST)
    return jnp.einsum('isgbc,ibe->isgec', partial_a, incoming[:, 1], precision=HIGHEST)

def outgoing(tensors, incoming):
    partial_c = jnp.einsum('isabc,icd->isabd', tensors, incoming[:, 2], precision=HIGHEST)
    both_bc = jnp.einsum('isabd,ibe->isaed', partial_c, incoming[:, 1], precision=HIGHEST)
    leg_zero = jnp.einsum('isaed,isfed->iaf', both_bc, tensors, precision=HIGHEST)
    both_ac = jnp.einsum('isabd,iag->isgbd', partial_c, incoming[:, 0], precision=HIGHEST)
    leg_one = jnp.einsum('isgbd,isghd->ibh', both_ac, tensors, precision=HIGHEST)
    both_ab = weighted(tensors, incoming)
    leg_two = jnp.einsum('isgec,isgek->ick', both_ab, tensors, precision=HIGHEST)
    return jnp.stack([leg_zero, leg_one, leg_two], axis=1)

def normalized(leg_terms):
    trace_sum = jnp.trace(leg_terms, axis1=2, axis2=3)
    return leg_terms.shape[-1] * leg_terms / trace_sum[:, :, None, None]

def sources(local_src, send_list, send_dest, per_region, capacity, columns):
    site_count = local_src.shape[0]
    region = (jnp.arange(site_count, dtype=jnp.int32) // SITES_DEV)[:, None]
    region_count = send_dest.shape[0]
    remote = local_src - per_region
    sender = jnp.clip(remote // capacity, 0, region_count - 1).astype(jnp.int32)
    wanted = region * capacity + remote % capacity
    dest_rows = send_dest[sender]
    matched = dest_rows == wanted[:, :, None]
    position = lax.optimization_barrier(jnp.sum(jnp.where(matched, jnp.arange(columns, dtype=jnp.int32), 0), axis=2)).astype(jnp.int32)
    remote_index = sender * per_region + send_list[sender * columns + position]
    local_index = region * per_region + local_src
    absent = local_src == per_region + region_count * capacity
    source_index = jnp.where(local_src < per_region, local_index, jnp.where(absent, 0, remote_index))
    return (source_index.astype(jnp.int32), absent)

def reference(site_tensors, projectors, gate_matrix, recv_src, cut_list, cut_dest, gate_src, gate_list, gate_dest):
    site_count = site_tensors.shape[0]
    bond_dim = site_tensors.shape[2]
    tensors = site_tensors.reshape(N_REGION, SITES_DEV, 2, bond_dim, bond_dim, bond_dim)
    msg_index, msg_absent = sources(recv_src, cut_list, cut_dest, 3 * SITES_DEV, CAP, CUT_MAX)
    boundary = jnp.zeros((bond_dim, bond_dim), jnp.float32).at[0, 0].set(bond_dim)
    identity = jnp.eye(bond_dim, dtype=jnp.float32)
    absent_mask = msg_absent[:, :, None, None]
    incoming = jnp.where(absent_mask, boundary, identity)

    def sweep_block(inputs):
        return normalized(outgoing(inputs[0], inputs[1]))
    for sweep_index in range(SWEEPS):
        blocks = incoming.reshape(N_REGION, SITES_DEV, 3, bond_dim, bond_dim)
        fresh_msgs = lax.map(sweep_block, (tensors, blocks))
        fresh_msgs = fresh_msgs.reshape(site_count * 3, bond_dim, bond_dim)
        incoming = jnp.where(absent_mask, boundary, fresh_msgs[msg_index])
    messages = incoming.reshape(site_count, 3, bond_dim * bond_dim)

    def factor_block(inputs):
        block_tensors, block_incoming, block_projectors = inputs
        weights = weighted(block_tensors, block_incoming).astype(jnp.bfloat16)
        shaped = block_projectors.reshape(SITES_DEV, 2, bond_dim, bond_dim, bond_dim).astype(jnp.float32)
        factor = jnp.einsum('iygec,isnge->iycsn', weights.astype(jnp.float32), shaped, precision=HIGHEST)
        return factor.astype(jnp.bfloat16)
    factors = lax.map(factor_block, (tensors, incoming.reshape(N_REGION, SITES_DEV, 3, bond_dim, bond_dim), projectors.reshape(N_REGION, SITES_DEV, 2, bond_dim, bond_dim * bond_dim)))
    factors = factors.reshape(site_count, 2, bond_dim, 2, bond_dim)
    gate_index, gate_absent = sources(gate_src[:, None], gate_list, gate_dest, SITES_DEV, GCAP, GCUT)
    no_gate = gate_absent[:, 0]
    partners = jnp.where(no_gate[:, None, None, None, None], jnp.zeros((), jnp.bfloat16), factors[gate_index[:, 0]])

    def update_block(inputs):
        block_tensors, block_partner, block_none = inputs
        mixing = jnp.einsum('ajby,iycjn->iabcn', gate_matrix, block_partner.astype(jnp.float32), precision=HIGHEST)
        updated = jnp.einsum('ibuvc,iabcn->iauvn', block_tensors, mixing, precision=HIGHEST)
        mean_sq = lax.optimization_barrier(jnp.mean(updated * updated, axis=(1, 2, 3, 4)))
        updated = updated / jnp.sqrt(mean_sq + EPSILON)[:, None, None, None, None]
        return jnp.where(block_none[:, None, None, None, None], block_tensors, updated)
    new_sites = lax.map(update_block, (tensors, partners.reshape(N_REGION, SITES_DEV, 2, bond_dim, 2, bond_dim), no_gate.reshape(N_REGION, SITES_DEV)))
    new_sites = new_sites.reshape(site_count, 2, bond_dim, bond_dim * bond_dim)
    return (new_sites, messages)
```

```python
import functools

import jax
import jax.numpy as jnp
from jax import lax
from jax.experimental import pallas as pl
from jax.experimental.pallas import tpu as pltpu
from jax.sharding import PartitionSpec as P

SWEEPS = 2
CAP = 4
GCAP = 1
EPSILON = 1e-06
HIGH = lax.Precision.HIGH
VMEM = pl.BlockSpec(memory_space=pltpu.VMEM)
SMEM = pl.BlockSpec(memory_space=pltpu.SMEM)
MESH = pl.DeviceIdType.MESH


def greet(regions):
    me = lax.axis_index("region")
    core = lax.axis_index("blk")
    barrier = pltpu.get_barrier_semaphore()
    pl.semaphore_signal(barrier, inc=1, device_id=(me, 1 - core), device_id_type=MESH)

    def hello(step, carry):
        other = lax.rem(me + step, regions)
        pl.semaphore_signal(barrier, inc=1, device_id=(other, core), device_id_type=MESH)
        return carry

    lax.fori_loop(1, regions, hello, 0)
    pl.semaphore_wait(barrier, regions)


def sweep_kernel(
    regions,
    send_index,
    recv_src,
    partial,
    edge,
    out,
    mate,
    lookup,
    outbox,
    arrived,
    mate_sem,
    send_sem,
    recv_sem,
):
    me = lax.axis_index("region")
    core = lax.axis_index("blk")
    messages = partial.shape[0]
    greet(regions)
    swap = pltpu.make_async_remote_copy(
        src_ref=partial,
        dst_ref=mate,
        send_sem=mate_sem.at[0],
        recv_sem=mate_sem.at[1],
        device_id=(me, 1 - core),
        device_id_type=MESH,
    )
    swap.start()
    swap.wait()
    total = partial[...] + mate[...]
    side = 32
    flat = 128 * lax.broadcasted_iota(jnp.int32, (1, 8, 128), 1) + lax.broadcasted_iota(
        jnp.int32, (1, 8, 128), 2
    )
    on_diagonal = (flat // side) == (flat % side)
    trace = jnp.sum(jnp.where(on_diagonal, total, 0.0), axis=(1, 2), keepdims=True)
    lookup[pl.ds(0, messages)] = side * total / trace

    def fill(entry, carry):
        outbox[entry // CAP, entry % CAP] = lookup[send_index[entry]]
        return carry

    lax.fori_loop(0, regions * CAP, fill, 0)

    def remote(other, slot):
        return pltpu.make_async_remote_copy(
            src_ref=outbox.at[other],
            dst_ref=arrived.at[slot],
            send_sem=send_sem.at[other],
            recv_sem=recv_sem.at[slot],
            device_id=(other, core),
            device_id_type=MESH,
        )

    def send(step, carry):
        other = lax.rem(me + step, regions)
        remote(other, me).start()
        return carry

    lax.fori_loop(1, regions, send, 0)
    arrived[me] = outbox[me]

    def collect(step, carry):
        other = lax.rem(me + step, regions)
        remote(other, me).wait_send()
        remote(other, other).wait_recv()
        return carry

    lax.fori_loop(1, regions, collect, 0)
    lookup[pl.ds(messages, regions * CAP)] = arrived[...].reshape(regions * CAP, 8, 128)
    lookup[messages + regions * CAP] = edge[...]

    def pick(entry, carry):
        out[entry] = lookup[recv_src[entry]]
        return carry

    lax.fori_loop(0, messages, pick, 0)


def exchange_messages(regions, send_index, recv_src, partial, edge):
    messages = partial.shape[0]
    return pl.pallas_call(
        functools.partial(sweep_kernel, regions),
        out_shape=jax.ShapeDtypeStruct((messages, 8, 128), jnp.float32),
        in_specs=[SMEM, SMEM, VMEM, VMEM],
        out_specs=VMEM,
        scratch_shapes=[
            pltpu.VMEM((messages, 8, 128), jnp.float32),
            pltpu.VMEM((messages + regions * CAP + 1, 8, 128), jnp.float32),
            pltpu.VMEM((regions, CAP, 8, 128), jnp.float32),
            pltpu.VMEM((regions, CAP, 8, 128), jnp.float32),
            pltpu.SemaphoreType.DMA((2,)),
            pltpu.SemaphoreType.DMA((regions,)),
            pltpu.SemaphoreType.DMA((regions,)),
        ],
        compiler_params=pltpu.CompilerParams(
            collective_id=0, has_side_effects=True, vmem_limit_bytes=32 * 2**20
        ),
    )(send_index, recv_src, partial, edge)


def factor_kernel(
    regions,
    send_index,
    gate_src,
    factor,
    out,
    lookup,
    outbox,
    arrived,
    half,
    mate_sem,
    send_sem,
    recv_sem,
):
    me = lax.axis_index("region")
    core = lax.axis_index("blk")
    sites = factor.shape[0]
    greet(regions)
    lookup[pl.ds(0, sites)] = factor[...]

    def fill(entry, carry):
        outbox[entry] = lookup[send_index[entry]]
        return carry

    lax.fori_loop(0, regions, fill, 0)

    def remote(other, slot):
        return pltpu.make_async_remote_copy(
            src_ref=outbox.at[other],
            dst_ref=arrived.at[slot],
            send_sem=send_sem.at[other],
            recv_sem=recv_sem.at[slot],
            device_id=(other, core),
            device_id_type=MESH,
        )

    def send(step, carry):
        other = lax.rem(me + step, regions)
        remote(other, me).start()
        return carry

    lax.fori_loop(1, regions, send, 0)
    arrived[me] = outbox[me]

    def collect(step, carry):
        other = lax.rem(me + step, regions)
        remote(other, me).wait_send()
        remote(other, other).wait_recv()
        return carry

    lax.fori_loop(1, regions, collect, 0)
    lookup[pl.ds(sites, regions)] = arrived[...]
    lookup[sites + regions] = jnp.zeros_like(lookup[0])

    def pick(entry, carry):
        half[entry] = lookup[gate_src[entry]]
        return carry

    lax.fori_loop(0, sites, pick, 0)
    out[core] = half[...]
    swap = pltpu.make_async_remote_copy(
        src_ref=half,
        dst_ref=out.at[core],
        send_sem=mate_sem.at[0],
        recv_sem=mate_sem.at[1],
        device_id=(me, 1 - core),
        device_id_type=MESH,
    )
    swap.start()
    swap.wait()


def exchange_factors(regions, send_index, gate_src, factor):
    sites = factor.shape[0]
    tile = factor.shape[1:]
    return pl.pallas_call(
        functools.partial(factor_kernel, regions),
        out_shape=jax.ShapeDtypeStruct((2, sites) + tile, factor.dtype),
        in_specs=[SMEM, SMEM, VMEM],
        out_specs=VMEM,
        scratch_shapes=[
            pltpu.VMEM((sites + regions + 1,) + tile, factor.dtype),
            pltpu.VMEM((regions,) + tile, factor.dtype),
            pltpu.VMEM((regions,) + tile, factor.dtype),
            pltpu.VMEM((sites,) + tile, factor.dtype),
            pltpu.SemaphoreType.DMA((2,)),
            pltpu.SemaphoreType.DMA((regions,)),
            pltpu.SemaphoreType.DMA((regions,)),
        ],
        compiler_params=pltpu.CompilerParams(
            collective_id=1, has_side_effects=True, vmem_limit_bytes=32 * 2**20
        ),
    )(send_index, gate_src, factor)


def split(value):
    high = value.astype(jnp.bfloat16)
    low = (value - high.astype(jnp.float32)).astype(jnp.bfloat16)
    return high, low


def dot3(left, right):
    left_high, left_low = left
    right_high, right_low = right
    dot = functools.partial(jnp.dot, preferred_element_type=jnp.float32)
    return dot(left_high, right_high) + (dot(left_low, right_high) + dot(left_high, right_low))


def update_kernel(
    tensors, mixing, keep, out, own, outbox, inbox, squares, mate_squares, send_sem, recv_sem
):
    me = lax.axis_index("region")
    core = lax.axis_index("blk")
    sites, bond, width = tensors.shape
    pieces = width // 128
    barrier = pltpu.get_barrier_semaphore()
    pl.semaphore_signal(barrier, inc=1, device_id=(me, 1 - core), device_id_type=MESH)
    pl.semaphore_wait(barrier, 1)

    def remote(site):
        return pltpu.make_async_remote_copy(
            src_ref=outbox.at[site],
            dst_ref=inbox.at[site],
            send_sem=send_sem.at[site],
            recv_sem=recv_sem.at[site],
            device_id=(me, 1 - core),
            device_id_type=MESH,
        )

    def multiply(site, carry):
        stacked = jnp.concatenate(
            [tensors[site, :, 128 * j : 128 * (j + 1)] for j in range(pieces)], axis=0
        )
        product = dot3(split(stacked), split(mixing[site]))
        for j in range(pieces):
            rows = product[bond * j : bond * (j + 1)]
            outbox[site, :, 128 * j : 128 * (j + 1)] = rows[:, :128].astype(jnp.bfloat16)
            own[site, :, 128 * j : 128 * (j + 1)] = rows[:, 128:]
        remote(site).start()
        return carry

    lax.fori_loop(0, sites, multiply, 0)

    def gather(site, carry):
        remote(site).wait()
        total = own[site] + inbox[site].astype(jnp.float32)
        own[site] = total
        squares[site] = jnp.sum((total * total).reshape(4, 8, width), axis=0)
        return carry

    lax.fori_loop(0, sites, gather, 0)
    folded = jnp.sum(squares[...], axis=(1, 2), keepdims=True)
    mate_squares[0] = jnp.broadcast_to(folded, (sites, 8, 128))
    swap = pltpu.make_async_remote_copy(
        src_ref=mate_squares.at[0],
        dst_ref=mate_squares.at[1],
        send_sem=send_sem.at[sites],
        recv_sem=recv_sem.at[sites],
        device_id=(me, 1 - core),
        device_id_type=MESH,
    )
    swap.start()
    swap.wait()

    def finish(site, carry):
        mean = (mate_squares[0, site] + mate_squares[1, site])[0:1, 0:1] / (2 * bond**3)
        updated = own[site] * lax.rsqrt(mean + EPSILON)
        out[site] = jnp.where(keep[site] > 0, tensors[site], updated)
        return carry

    lax.fori_loop(0, sites, finish, 0)


def update(tensors, mixing, keep):
    sites, bond, width = tensors.shape
    return pl.pallas_call(
        update_kernel,
        out_shape=jax.ShapeDtypeStruct(tensors.shape, jnp.float32),
        in_specs=[VMEM, VMEM, SMEM],
        out_specs=VMEM,
        scratch_shapes=[
            pltpu.VMEM(tensors.shape, jnp.float32),
            pltpu.VMEM(tensors.shape, jnp.bfloat16),
            pltpu.VMEM(tensors.shape, jnp.bfloat16),
            pltpu.VMEM((sites, 8, width), jnp.float32),
            pltpu.VMEM((2, sites, 8, 128), jnp.float32),
            pltpu.SemaphoreType.DMA((sites + 1,)),
            pltpu.SemaphoreType.DMA((sites + 1,)),
        ],
        compiler_params=pltpu.CompilerParams(
            collective_id=2, has_side_effects=True, vmem_limit_bytes=32 * 2**20
        ),
    )(tensors, mixing, keep)


def outgoing(tensors, incoming):
    on_a = jnp.einsum("iabc,iag->igbc", tensors, incoming[:, 0], precision=HIGH)
    on_b = jnp.einsum("iabc,ibg->iagc", tensors, incoming[:, 1], precision=HIGH)
    on_c = jnp.einsum("iabc,icg->iabg", tensors, incoming[:, 2], precision=HIGH)
    leg_zero = jnp.einsum("iabc,ifbc->iaf", on_b, on_c, precision=HIGH)
    leg_one = jnp.einsum("iabc,iafc->ibf", on_a, on_c, precision=HIGH)
    leg_two = jnp.einsum("iabc,iabf->icf", on_a, on_b, precision=HIGH)
    return jnp.stack([leg_zero, leg_one, leg_two], axis=1)


def slots(entries, dest_row, count):
    matched = dest_row[None, :] == jnp.arange(count, dtype=jnp.int32)[:, None]
    return jnp.sum(jnp.where(matched, entries[None, :], 0), axis=1).astype(jnp.int32)


def shards(
    site_tensors,
    projectors,
    gate_matrix,
    recv_src,
    cut_list,
    cut_dest,
    gate_src,
    gate_list,
    gate_dest,
):
    site_count = site_tensors.shape[0]
    bond_dim = site_tensors.shape[2]
    regions = lax.axis_size("region")
    my_region = lax.axis_index("region")
    my_spin = lax.axis_index("blk")
    tensors = site_tensors.reshape(site_count, bond_dim, bond_dim, bond_dim)
    boundary = jnp.zeros((bond_dim, bond_dim), jnp.float32).at[0, 0].set(bond_dim)
    identity = jnp.eye(bond_dim, dtype=jnp.float32)
    msg_none = 3 * site_count + regions * CAP
    incoming = jnp.where((recv_src == msg_none)[:, :, None, None], boundary, identity)
    edge = boundary.reshape(8, 128)
    own_dest = lax.dynamic_index_in_dim(cut_dest, my_region, 0, keepdims=False)
    own_gate = lax.dynamic_index_in_dim(gate_dest, my_region, 0, keepdims=False)
    send_index = slots(cut_list, own_dest, regions * CAP)
    gate_index = slots(gate_list, own_gate, regions * GCAP)
    flat_src = recv_src.reshape(-1)
    for _ in range(SWEEPS):
        partial = outgoing(tensors, incoming).reshape(3 * site_count, 8, 128)
        flat = exchange_messages(regions, send_index, flat_src, partial, edge)
        incoming = flat.reshape(site_count, 3, bond_dim, bond_dim)
    messages = flat.reshape(site_count, 3, bond_dim * bond_dim)
    half = jnp.einsum("iabc,iag->igbc", tensors, incoming[:, 0], precision=HIGH)
    weights = (
        jnp.einsum("igbc,ibe->igec", half, incoming[:, 1], precision=HIGH)
        .astype(jnp.bfloat16)
        .reshape(site_count, bond_dim * bond_dim, bond_dim)
    )
    factor = jnp.einsum(
        "ikc,isnk->icsn", weights, projectors, preferred_element_type=jnp.float32
    ).astype(jnp.bfloat16)
    factor = factor.reshape(site_count, 2 * bond_dim * bond_dim // 128, 128)
    both = exchange_factors(regions, gate_index, gate_src, factor)
    partners = both.reshape(2, site_count, bond_dim, 2, bond_dim)
    own_gate_rows = lax.dynamic_index_in_dim(gate_matrix, my_spin, 2, keepdims=False)
    ordered = jnp.stack(
        [
            lax.dynamic_index_in_dim(own_gate_rows, 1 - my_spin, 0, keepdims=False),
            lax.dynamic_index_in_dim(own_gate_rows, my_spin, 0, keepdims=False),
        ]
    )
    mixing = jnp.sum(
        ordered.transpose(0, 2, 1)[:, :, None, None, :, None]
        * partners.astype(jnp.float32)[None],
        axis=(1, 4),
    )
    copies = 128 // bond_dim
    eye = jnp.eye(copies, dtype=jnp.float32)
    blocks = jnp.einsum("ticn,pq->ipctqn", mixing, eye, precision=lax.Precision.HIGHEST)
    blocks = blocks.reshape(site_count, 128, 256)
    keep = (gate_src == site_count + regions * GCAP).astype(jnp.int32)
    new_sites = update(site_tensors.reshape(site_count, bond_dim, -1), blocks, keep)
    return (new_sites.reshape(site_tensors.shape), messages)


def solution(mesh):
    return jax.shard_map(
        shards,
        mesh=mesh,
        in_specs=(
            P("region", "blk", None, None),
            P("region", None, None, None),
            P(),
            P("region", None),
            P("region"),
            P(),
            P("region"),
            P("region"),
            P(),
        ),
        out_specs=(P("region", "blk", None, None), P("region", None, None)),
        check_vma=False,
    )
```

```python
import functools

import jax
import jax.numpy as jnp
from jax import lax
from jax.experimental import pallas as pl
from jax.experimental.pallas import tpu as pltpu
from jax.sharding import PartitionSpec as P

SWEEPS = 2
CAP = 4
GCAP = 1
EPSILON = 1e-06
HIGH = lax.Precision.HIGH
VMEM = pl.BlockSpec(memory_space=pltpu.VMEM)
SMEM = pl.BlockSpec(memory_space=pltpu.SMEM)
MESH = pl.DeviceIdType.MESH


def greet(regions):
    me = lax.axis_index("region")
    core = lax.axis_index("blk")
    barrier = pltpu.get_barrier_semaphore()
    pl.semaphore_signal(barrier, inc=1, device_id=(me, 1 - core), device_id_type=MESH)

    def hello(step, carry):
        other = lax.rem(me + step, regions)
        pl.semaphore_signal(barrier, inc=1, device_id=(other, core), device_id_type=MESH)
        return carry

    lax.fori_loop(1, regions, hello, 0)
    pl.semaphore_wait(barrier, regions)


def sweep_kernel(
    regions,
    send_index,
    recv_src,
    partial,
    edge,
    out,
    mate,
    lookup,
    outbox,
    arrived,
    mate_sem,
    send_sem,
    recv_sem,
):
    me = lax.axis_index("region")
    core = lax.axis_index("blk")
    messages = partial.shape[0]
    greet(regions)
    swap = pltpu.make_async_remote_copy(
        src_ref=partial,
        dst_ref=mate,
        send_sem=mate_sem.at[0],
        recv_sem=mate_sem.at[1],
        device_id=(me, 1 - core),
        device_id_type=MESH,
    )
    swap.start()
    swap.wait()
    total = partial[...] + mate[...]
    side = 32
    flat = 128 * lax.broadcasted_iota(jnp.int32, (1, 8, 128), 1) + lax.broadcasted_iota(
        jnp.int32, (1, 8, 128), 2
    )
    on_diagonal = (flat // side) == (flat % side)
    trace = jnp.sum(jnp.where(on_diagonal, total, 0.0), axis=(1, 2), keepdims=True)
    lookup[pl.ds(0, messages)] = side * total / trace

    def fill(entry, carry):
        outbox[entry // CAP, entry % CAP] = lookup[send_index[entry]]
        return carry

    lax.fori_loop(0, regions * CAP, fill, 0)

    def remote(other, slot):
        return pltpu.make_async_remote_copy(
            src_ref=outbox.at[other],
            dst_ref=arrived.at[slot],
            send_sem=send_sem.at[other],
            recv_sem=recv_sem.at[slot],
            device_id=(other, core),
            device_id_type=MESH,
        )

    def send(step, carry):
        other = lax.rem(me + step, regions)
        remote(other, me).start()
        return carry

    lax.fori_loop(1, regions, send, 0)
    arrived[me] = outbox[me]

    def collect(step, carry):
        other = lax.rem(me + step, regions)
        remote(other, me).wait_send()
        remote(other, other).wait_recv()
        return carry

    lax.fori_loop(1, regions, collect, 0)
    lookup[pl.ds(messages, regions * CAP)] = arrived[...].reshape(regions * CAP, 8, 128)
    lookup[messages + regions * CAP] = edge[...]

    def pick(entry, carry):
        out[entry] = lookup[recv_src[entry]]
        return carry

    lax.fori_loop(0, messages, pick, 0)


def exchange_messages(regions, send_index, recv_src, partial, edge):
    messages = partial.shape[0]
    return pl.pallas_call(
        functools.partial(sweep_kernel, regions),
        out_shape=jax.ShapeDtypeStruct((messages, 8, 128), jnp.float32),
        in_specs=[SMEM, SMEM, VMEM, VMEM],
        out_specs=VMEM,
        scratch_shapes=[
            pltpu.VMEM((messages, 8, 128), jnp.float32),
            pltpu.VMEM((messages + regions * CAP + 1, 8, 128), jnp.float32),
            pltpu.VMEM((regions, CAP, 8, 128), jnp.float32),
            pltpu.VMEM((regions, CAP, 8, 128), jnp.float32),
            pltpu.SemaphoreType.DMA((2,)),
            pltpu.SemaphoreType.DMA((regions,)),
            pltpu.SemaphoreType.DMA((regions,)),
        ],
        compiler_params=pltpu.CompilerParams(
            collective_id=0, has_side_effects=True, vmem_limit_bytes=32 * 2**20
        ),
    )(send_index, recv_src, partial, edge)


def factor_kernel(
    regions,
    send_index,
    gate_src,
    factor,
    out,
    lookup,
    outbox,
    arrived,
    half,
    mate_sem,
    send_sem,
    recv_sem,
):
    me = lax.axis_index("region")
    core = lax.axis_index("blk")
    sites = factor.shape[0]
    greet(regions)
    lookup[pl.ds(0, sites)] = factor[...]

    def fill(entry, carry):
        outbox[entry] = lookup[send_index[entry]]
        return carry

    lax.fori_loop(0, regions, fill, 0)

    def remote(other, slot):
        return pltpu.make_async_remote_copy(
            src_ref=outbox.at[other],
            dst_ref=arrived.at[slot],
            send_sem=send_sem.at[other],
            recv_sem=recv_sem.at[slot],
            device_id=(other, core),
            device_id_type=MESH,
        )

    def send(step, carry):
        other = lax.rem(me + step, regions)
        remote(other, me).start()
        return carry

    lax.fori_loop(1, regions, send, 0)
    arrived[me] = outbox[me]

    def collect(step, carry):
        other = lax.rem(me + step, regions)
        remote(other, me).wait_send()
        remote(other, other).wait_recv()
        return carry

    lax.fori_loop(1, regions, collect, 0)
    lookup[pl.ds(sites, regions)] = arrived[...]
    lookup[sites + regions] = jnp.zeros_like(lookup[0])

    def pick(entry, carry):
        half[entry] = lookup[gate_src[entry]]
        return carry

    lax.fori_loop(0, sites, pick, 0)
    out[core] = half[...]
    swap = pltpu.make_async_remote_copy(
        src_ref=half,
        dst_ref=out.at[core],
        send_sem=mate_sem.at[0],
        recv_sem=mate_sem.at[1],
        device_id=(me, 1 - core),
        device_id_type=MESH,
    )
    swap.start()
    swap.wait()


def exchange_factors(regions, send_index, gate_src, factor):
    sites = factor.shape[0]
    tile = factor.shape[1:]
    return pl.pallas_call(
        functools.partial(factor_kernel, regions),
        out_shape=jax.ShapeDtypeStruct((2, sites) + tile, factor.dtype),
        in_specs=[SMEM, SMEM, VMEM],
        out_specs=VMEM,
        scratch_shapes=[
            pltpu.VMEM((sites + regions + 1,) + tile, factor.dtype),
            pltpu.VMEM((regions,) + tile, factor.dtype),
            pltpu.VMEM((regions,) + tile, factor.dtype),
            pltpu.VMEM((sites,) + tile, factor.dtype),
            pltpu.SemaphoreType.DMA((2,)),
            pltpu.SemaphoreType.DMA((regions,)),
            pltpu.SemaphoreType.DMA((regions,)),
        ],
        compiler_params=pltpu.CompilerParams(
            collective_id=1, has_side_effects=True, vmem_limit_bytes=32 * 2**20
        ),
    )(send_index, gate_src, factor)


def split(value):
    high = value.astype(jnp.bfloat16)
    low = (value - high.astype(jnp.float32)).astype(jnp.bfloat16)
    return high, low


def dot3(left, right):
    left_high, left_low = left
    right_high, right_low = right
    dot = functools.partial(jnp.dot, preferred_element_type=jnp.float32)
    return dot(left_high, right_high) + (dot(left_low, right_high) + dot(left_high, right_low))


def update_kernel(
    tensors, mixing, keep, out, own, outbox, inbox, squares, mate_squares, send_sem, recv_sem
):
    me = lax.axis_index("region")
    core = lax.axis_index("blk")
    sites, bond, width = tensors.shape
    pieces = width // 128
    barrier = pltpu.get_barrier_semaphore()
    pl.semaphore_signal(barrier, inc=1, device_id=(me, 1 - core), device_id_type=MESH)
    pl.semaphore_wait(barrier, 1)

    def remote(site):
        return pltpu.make_async_remote_copy(
            src_ref=outbox.at[site],
            dst_ref=inbox.at[site],
            send_sem=send_sem.at[site],
            recv_sem=recv_sem.at[site],
            device_id=(me, 1 - core),
            device_id_type=MESH,
        )

    def multiply(site, carry):
        stacked = jnp.concatenate(
            [tensors[site, :, 128 * j : 128 * (j + 1)] for j in range(pieces)], axis=0
        )
        product = dot3(split(stacked), split(mixing[site]))
        for j in range(pieces):
            rows = product[bond * j : bond * (j + 1)]
            outbox[site, :, 128 * j : 128 * (j + 1)] = rows[:, :128].astype(jnp.bfloat16)
            own[site, :, 128 * j : 128 * (j + 1)] = rows[:, 128:]
        remote(site).start()
        return carry

    lax.fori_loop(0, sites, multiply, 0)

    def gather(site, carry):
        remote(site).wait()
        total = own[site] + inbox[site].astype(jnp.float32)
        own[site] = total
        squares[site] = jnp.sum((total * total).reshape(4, 8, width), axis=0)
        return carry

    lax.fori_loop(0, sites, gather, 0)
    folded = jnp.sum(squares[...], axis=(1, 2), keepdims=True)
    mate_squares[0] = jnp.broadcast_to(folded, (sites, 8, 128))
    swap = pltpu.make_async_remote_copy(
        src_ref=mate_squares.at[0],
        dst_ref=mate_squares.at[1],
        send_sem=send_sem.at[sites],
        recv_sem=recv_sem.at[sites],
        device_id=(me, 1 - core),
        device_id_type=MESH,
    )
    swap.start()
    swap.wait()

    def finish(site, carry):
        mean = (mate_squares[0, site] + mate_squares[1, site])[0:1, 0:1] / (2 * bond**3)
        updated = own[site] * lax.rsqrt(mean + EPSILON)
        out[site] = jnp.where(keep[site] > 0, tensors[site], updated)
        return carry

    lax.fori_loop(0, sites, finish, 0)


def update(tensors, mixing, keep):
    sites, bond, width = tensors.shape
    return pl.pallas_call(
        update_kernel,
        out_shape=jax.ShapeDtypeStruct(tensors.shape, jnp.float32),
        in_specs=[VMEM, VMEM, SMEM],
        out_specs=VMEM,
        scratch_shapes=[
            pltpu.VMEM(tensors.shape, jnp.float32),
            pltpu.VMEM(tensors.shape, jnp.bfloat16),
            pltpu.VMEM(tensors.shape, jnp.bfloat16),
            pltpu.VMEM((sites, 8, width), jnp.float32),
            pltpu.VMEM((2, sites, 8, 128), jnp.float32),
            pltpu.SemaphoreType.DMA((sites + 1,)),
            pltpu.SemaphoreType.DMA((sites + 1,)),
        ],
        compiler_params=pltpu.CompilerParams(
            collective_id=2, has_side_effects=True, vmem_limit_bytes=32 * 2**20
        ),
    )(tensors, mixing, keep)


def contract(left, right, dims):
    dot = functools.partial(
        lax.dot_general,
        dimension_numbers=(dims, ((), ())),
        preferred_element_type=jnp.float32,
    )
    return dot(left[0], right[0]) + (dot(left[1], right[0]) + dot(left[0], right[1]))


def chunks(rows):
    return jnp.concatenate(
        [rows[:, 128 * j : 128 * (j + 1)] for j in range(rows.shape[1] // 128)], axis=0
    )


def unchunk(stacked, bond):
    return jnp.concatenate(
        [stacked[bond * j : bond * (j + 1)] for j in range(stacked.shape[0] // bond)], axis=1
    )


def swap_axes(stacked, source, target, bond):
    per = 128 // bond
    groups = bond // per
    source[...] = stacked
    lane = lax.broadcasted_iota(jnp.int32, (groups * groups, 128), 1) // bond
    taken = [
        jnp.concatenate(
            [source[pl.ds(per * k + q, groups, stride=bond), :] for k in range(groups)], axis=0
        )
        for q in range(per)
    ]
    for p in range(per):
        merged = taken[p]
        for q in range(per):
            if q != p:
                moved = pltpu.roll(taken[q], (bond * (q - p)) % 128, 1)
                merged = jnp.where(lane == q, moved, merged)
        for k in range(groups):
            target[pl.ds(bond * k + p, groups, stride=per), :] = merged[
                groups * k : groups * (k + 1)
            ]
    return target[...]


def diagonal(matrix):
    bond = matrix.shape[0]
    per = 128 // bond
    wide = jnp.concatenate([matrix] * per, axis=1)
    tall = jnp.concatenate([wide] * per, axis=0)
    row = lax.broadcasted_iota(jnp.int32, (128, 128), 0) // bond
    column = lax.broadcasted_iota(jnp.int32, (128, 128), 1) // bond
    return jnp.where(row == column, tall, 0.0)


def outgoing_kernel(tensors, incoming, out, source_a, target_a, source_b, target_b, source_c, target_c):
    sites, bond, _ = tensors.shape
    row = lax.broadcasted_iota(jnp.int32, (128, 128), 0) // bond
    column = lax.broadcasted_iota(jnp.int32, (128, 128), 1) // bond
    same = row == column
    rows, inner, outer = ((1,), (0,)), ((1,), (1,)), ((0,), (0,))

    def one(site, carry):
        wide = tensors[site]
        plain = chunks(wide)
        swapped = swap_axes(plain, source_a, target_a, bond)
        swapped_wide = unchunk(swapped, bond)
        left = split(incoming[site, 0])
        right = split(incoming[site, 1])
        vertical = split(diagonal(incoming[site, 2]))
        on_a = contract(left, split(wide), outer)
        on_b = contract(right, split(swapped_wide), outer)
        on_a_stacked = chunks(on_a)
        on_a_swapped = unchunk(swap_axes(on_a_stacked, source_b, target_b, bond), bond)
        on_b_stacked = swap_axes(chunks(on_b), source_c, target_c, bond)
        on_b_swapped = unchunk(on_b_stacked, bond)
        on_c = unchunk(contract(split(plain), vertical, rows), bond)
        on_c_swapped = unchunk(contract(split(swapped), vertical, rows), bond)
        out[site, 0] = contract(split(on_b_swapped), split(on_c), inner)
        out[site, 1] = contract(split(on_a_swapped), split(on_c_swapped), inner)
        crossed = contract(split(on_a_stacked), split(on_b_stacked), outer)
        crossed = jnp.where(same, crossed, 0.0)
        folded = sum(crossed[bond * p : bond * (p + 1)] for p in range(128 // bond))
        folded = folded + pltpu.roll(folded, 64, 1)
        folded = folded + pltpu.roll(folded, 32, 1)
        out[site, 2] = folded[:, :bond]
        return carry

    lax.fori_loop(0, sites, one, 0)


def outgoing(tensors, incoming):
    sites, bond, width = tensors.shape
    return pl.pallas_call(
        outgoing_kernel,
        out_shape=jax.ShapeDtypeStruct((sites, 3, bond, bond), jnp.float32),
        in_specs=[VMEM, VMEM],
        out_specs=VMEM,
        scratch_shapes=[pltpu.VMEM((bond * width // 128, 128), jnp.float32)] * 6,
        compiler_params=pltpu.CompilerParams(vmem_limit_bytes=32 * 2**20),
    )(tensors, incoming)


def slots(entries, dest_row, count):
    matched = dest_row[None, :] == jnp.arange(count, dtype=jnp.int32)[:, None]
    return jnp.sum(jnp.where(matched, entries[None, :], 0), axis=1).astype(jnp.int32)


def shards(
    site_tensors,
    projectors,
    gate_matrix,
    recv_src,
    cut_list,
    cut_dest,
    gate_src,
    gate_list,
    gate_dest,
):
    site_count = site_tensors.shape[0]
    bond_dim = site_tensors.shape[2]
    regions = lax.axis_size("region")
    my_region = lax.axis_index("region")
    my_spin = lax.axis_index("blk")
    tensors = site_tensors.reshape(site_count, bond_dim, bond_dim, bond_dim)
    flat_tensors = site_tensors.reshape(site_count, bond_dim, -1)
    boundary = jnp.zeros((bond_dim, bond_dim), jnp.float32).at[0, 0].set(bond_dim)
    identity = jnp.eye(bond_dim, dtype=jnp.float32)
    msg_none = 3 * site_count + regions * CAP
    incoming = jnp.where((recv_src == msg_none)[:, :, None, None], boundary, identity)
    edge = boundary.reshape(8, 128)
    own_dest = lax.dynamic_index_in_dim(cut_dest, my_region, 0, keepdims=False)
    own_gate = lax.dynamic_index_in_dim(gate_dest, my_region, 0, keepdims=False)
    send_index = slots(cut_list, own_dest, regions * CAP)
    gate_index = slots(gate_list, own_gate, regions * GCAP)
    flat_src = recv_src.reshape(-1)
    for _ in range(SWEEPS):
        partial = outgoing(flat_tensors, incoming).reshape(3 * site_count, 8, 128)
        flat = exchange_messages(regions, send_index, flat_src, partial, edge)
        incoming = flat.reshape(site_count, 3, bond_dim, bond_dim)
    messages = flat.reshape(site_count, 3, bond_dim * bond_dim)
    half = jnp.einsum("iabc,iag->igbc", tensors, incoming[:, 0], precision=HIGH)
    weights = (
        jnp.einsum("igbc,ibe->igec", half, incoming[:, 1], precision=HIGH)
        .astype(jnp.bfloat16)
        .reshape(site_count, bond_dim * bond_dim, bond_dim)
    )
    factor = jnp.einsum(
        "ikc,isnk->icsn", weights, projectors, preferred_element_type=jnp.float32
    ).astype(jnp.bfloat16)
    factor = factor.reshape(site_count, 2 * bond_dim * bond_dim // 128, 128)
    both = exchange_factors(regions, gate_index, gate_src, factor)
    partners = both.reshape(2, site_count, bond_dim, 2, bond_dim)
    own_gate_rows = lax.dynamic_index_in_dim(gate_matrix, my_spin, 2, keepdims=False)
    ordered = jnp.stack(
        [
            lax.dynamic_index_in_dim(own_gate_rows, 1 - my_spin, 0, keepdims=False),
            lax.dynamic_index_in_dim(own_gate_rows, my_spin, 0, keepdims=False),
        ]
    )
    mixing = jnp.sum(
        ordered.transpose(0, 2, 1)[:, :, None, None, :, None]
        * partners.astype(jnp.float32)[None],
        axis=(1, 4),
    )
    copies = 128 // bond_dim
    eye = jnp.eye(copies, dtype=jnp.float32)
    blocks = jnp.einsum("ticn,pq->ipctqn", mixing, eye, precision=lax.Precision.HIGHEST)
    blocks = blocks.reshape(site_count, 128, 256)
    keep = (gate_src == site_count + regions * GCAP).astype(jnp.int32)
    new_sites = update(site_tensors.reshape(site_count, bond_dim, -1), blocks, keep)
    return (new_sites.reshape(site_tensors.shape), messages)


def solution(mesh):
    return jax.shard_map(
        shards,
        mesh=mesh,
        in_specs=(
            P("region", "blk", None, None),
            P("region", None, None, None),
            P(),
            P("region", None),
            P("region"),
            P(),
            P("region"),
            P("region"),
            P(),
        ),
        out_specs=(P("region", "blk", None, None), P("region", None, None)),
        check_vma=False,
    )
```

```python
import functools

import jax
import jax.numpy as jnp
from jax import lax
from jax.experimental import pallas as pl
from jax.experimental.pallas import tpu as pltpu
from jax.sharding import PartitionSpec as P

SWEEPS = 2
CAP = 4
GCAP = 1
EPSILON = 1e-06
VMEM = pl.BlockSpec(memory_space=pltpu.VMEM)
SMEM = pl.BlockSpec(memory_space=pltpu.SMEM)
MESH = pl.DeviceIdType.MESH


def split(value):
    high = value.astype(jnp.bfloat16)
    low = (value - high.astype(jnp.float32)).astype(jnp.bfloat16)
    return high, low


def contract(left, right, dims):
    dot = functools.partial(
        lax.dot_general,
        dimension_numbers=(dims, ((), ())),
        preferred_element_type=jnp.float32,
    )
    return dot(left[0], right[0]) + (dot(left[1], right[0]) + dot(left[0], right[1]))


def chunks(rows):
    return jnp.concatenate(
        [rows[:, 128 * j : 128 * (j + 1)] for j in range(rows.shape[1] // 128)], axis=0
    )


def unchunk(stacked, bond):
    return jnp.concatenate(
        [stacked[bond * j : bond * (j + 1)] for j in range(stacked.shape[0] // bond)], axis=1
    )


def swap_axes(stacked, source, target, bond):
    per = 128 // bond
    groups = bond // per
    source[...] = stacked
    lane = lax.broadcasted_iota(jnp.int32, (groups * groups, 128), 1) // bond
    taken = [
        jnp.concatenate(
            [source[pl.ds(per * k + q, groups, stride=bond), :] for k in range(groups)], axis=0
        )
        for q in range(per)
    ]
    for p in range(per):
        merged = taken[p]
        for q in range(per):
            if q != p:
                moved = pltpu.roll(taken[q], (bond * (q - p)) % 128, 1)
                merged = jnp.where(lane == q, moved, merged)
        for k in range(groups):
            target[pl.ds(bond * k + p, groups, stride=per), :] = merged[
                groups * k : groups * (k + 1)
            ]
    return target[...]


def diagonal(matrix):
    bond = matrix.shape[0]
    per = 128 // bond
    wide = jnp.concatenate([matrix] * per, axis=1)
    tall = jnp.concatenate([wide] * per, axis=0)
    row = lax.broadcasted_iota(jnp.int32, (128, 128), 0) // bond
    column = lax.broadcasted_iota(jnp.int32, (128, 128), 1) // bond
    return jnp.where(row == column, tall, 0.0)


def slots(entries, dest_row, count):
    matched = dest_row[None, :] == jnp.arange(count, dtype=jnp.int32)[:, None]
    return jnp.sum(jnp.where(matched, entries[None, :], 0), axis=1).astype(jnp.int32)


def site_terms(tensors, current, site, swaps):
    bond = tensors.shape[1]
    rows, inner, outer = ((1,), (0,)), ((1,), (1,)), ((0,), (0,))
    wide = tensors[site]
    plain = chunks(wide)
    swapped = swap_axes(plain, swaps.at[0], swaps.at[1], bond)
    left = split(current[3 * site][:, :bond])
    right = split(current[3 * site + 1][:, :bond])
    vertical = split(diagonal(current[3 * site + 2][:, :bond]))
    on_a = contract(left, split(wide), outer)
    on_b = contract(right, split(unchunk(swapped, bond)), outer)
    on_a_stacked = chunks(on_a)
    on_a_swapped = unchunk(swap_axes(on_a_stacked, swaps.at[2], swaps.at[3], bond), bond)
    on_b_stacked = swap_axes(chunks(on_b), swaps.at[4], swaps.at[5], bond)
    on_b_swapped = unchunk(on_b_stacked, bond)
    on_c = unchunk(contract(split(plain), vertical, rows), bond)
    on_c_swapped = unchunk(contract(split(swapped), vertical, rows), bond)
    leg_zero = contract(split(on_b_swapped), split(on_c), inner)
    leg_one = contract(split(on_a_swapped), split(on_c_swapped), inner)
    crossed = contract(split(on_a_stacked), split(on_b_stacked), outer)
    crossed = jnp.where(same_block(bond), crossed, 0.0)
    folded = sum(crossed[bond * p : bond * (p + 1)] for p in range(128 // bond))
    return leg_zero, leg_one, fold_lanes(folded)[:, :bond]


def same_block(bond):
    row = lax.broadcasted_iota(jnp.int32, (128, 128), 0) // bond
    column = lax.broadcasted_iota(jnp.int32, (128, 128), 1) // bond
    return row == column


def fold_lanes(value):
    value = value + pltpu.roll(value, 64, 1)
    return value + pltpu.roll(value, 32, 1)


def flatten(matrix, scratch):
    bond = matrix.shape[0]
    per = 128 // bond
    scratch[...] = jnp.concatenate([matrix] * per, axis=1)
    lane = lax.broadcasted_iota(jnp.int32, (bond // per, 128), 1) // bond
    flat = scratch[pl.ds(0, bond // per, stride=per), :]
    for p in range(1, per):
        flat = jnp.where(lane == p, scratch[pl.ds(p, bond // per, stride=per), :], flat)
    return flat


def whole_kernel(
    regions,
    send_index,
    recv_src,
    gate_index,
    gate_src,
    gate,
    tensors,
    projectors,
    edge,
    new_out,
    msg_out,
    current,
    swaps,
    flats,
    partial,
    mate,
    lookup,
    outbox,
    arrived,
    factors,
    gate_outbox,
    gate_arrived,
    both,
    half,
    own,
    update_outbox,
    update_inbox,
    squares,
    norms,
    mate_sem,
    send_sem,
    recv_sem,
    gate_send_sem,
    gate_recv_sem,
    update_send_sem,
    update_recv_sem,
):
    me = lax.axis_index("region")
    core = lax.axis_index("blk")
    sites, bond, width = tensors.shape
    per = 128 // bond
    pieces = width // 128
    messages = 3 * sites
    none = messages + regions * CAP
    barrier = pltpu.get_barrier_semaphore()
    pl.semaphore_signal(barrier, inc=1, device_id=(me, 1 - core), device_id_type=MESH)

    def hello(step, carry):
        other = lax.rem(me + step, regions)
        pl.semaphore_signal(barrier, inc=1, device_id=(other, core), device_id_type=MESH)
        return carry

    lax.fori_loop(1, regions, hello, 0)

    def to_mate(source, target, index):
        return pltpu.make_async_remote_copy(
            src_ref=source,
            dst_ref=target,
            send_sem=mate_sem.at[2 * index],
            recv_sem=mate_sem.at[2 * index + 1],
            device_id=(me, 1 - core),
            device_id_type=MESH,
        )

    def unflatten(flat, entry):
        for p in range(per):
            moved = flat if p == 0 else pltpu.roll(flat, 128 - bond * p, 1)
            current[entry, pl.ds(p, bond // per, stride=per), :] = moved

    row = lax.broadcasted_iota(jnp.int32, (8, 128), 0)
    column = lax.broadcasted_iota(jnp.int32, (8, 128), 1)
    place = 128 * row + column
    diagonal_flat = (place // bond) == (place % bond)
    identity = jnp.where(diagonal_flat, 1.0, 0.0).astype(jnp.float32)

    def begin(entry, carry):
        unflatten(jnp.where(recv_src[entry] == none, edge[...], identity), entry)
        return carry

    lax.fori_loop(0, messages, begin, 0)

    for sweep in range(SWEEPS):

        def terms(site, carry, sweep=sweep):
            legs = site_terms(tensors, current, site, swaps)
            for leg in range(3):
                partial[sweep, 3 * site + leg] = flatten(legs[leg], flats.at[leg])
            return carry

        lax.fori_loop(0, sites, terms, 0)
        if sweep == 0:
            pl.semaphore_wait(barrier, regions)
        swap = to_mate(partial.at[sweep], mate.at[sweep], sweep)
        swap.start()
        swap.wait()
        total = partial[sweep] + mate[sweep]
        trace = jnp.sum(jnp.where(diagonal_flat[None], total, 0.0), axis=(1, 2), keepdims=True)
        lookup[pl.ds(0, messages)] = bond * total / trace

        def remote(other, slot, sweep=sweep):
            return pltpu.make_async_remote_copy(
                src_ref=outbox.at[sweep, other],
                dst_ref=arrived.at[sweep, slot],
                send_sem=send_sem.at[sweep, other],
                recv_sem=recv_sem.at[sweep, slot],
                device_id=(other, core),
                device_id_type=MESH,
            )

        def send(step, carry, sweep=sweep, remote=remote):
            other = lax.rem(me + step, regions)
            for slot in range(CAP):
                outbox[sweep, other, slot] = lookup[send_index[CAP * other + slot]]
            remote(other, me).start()
            return carry

        lax.fori_loop(1, regions, send, 0)
        arrived[sweep, me] = jnp.zeros_like(arrived[sweep, me])

        def collect(step, carry, remote=remote):
            other = lax.rem(me + step, regions)
            remote(other, me).wait_send()
            remote(other, other).wait_recv()
            return carry

        lax.fori_loop(1, regions, collect, 0)
        lookup[pl.ds(messages, regions * CAP)] = arrived[sweep].reshape(regions * CAP, 8, 128)
        lookup[none] = edge[...]

        def pick(site, carry, sweep=sweep):
            for leg in range(3):
                flat = lookup[recv_src[3 * site + leg]]
                unflatten(flat, 3 * site + leg)
                if sweep == SWEEPS - 1:
                    for j in range(pieces):
                        msg_out[site, leg : leg + 1, 128 * j : 128 * (j + 1)] = flat[j : j + 1]
            return carry

        lax.fori_loop(0, sites, pick, 0)

    outer = ((0,), (0,))
    same = same_block(bond)
    pack_lane = lax.broadcasted_iota(jnp.int32, (16, 128), 1) // bond

    def factor(site, carry):
        left = split(current[3 * site][:, :bond])
        right = split(current[3 * site + 1][:, :bond])
        on_a = contract(left, split(tensors[site]), outer)
        swapped = unchunk(swap_axes(chunks(on_a), swaps.at[0], swaps.at[1], bond), bond)
        weights = contract(right, split(swapped), outer)
        weights = weights.astype(jnp.bfloat16).astype(jnp.float32)
        tiles = [
            jnp.where(same, jnp.concatenate([weights[:, 128 * j : 128 * (j + 1)]] * per, axis=0), 0.0)
            for j in range(pieces)
        ]
        spread = jnp.concatenate(tiles, axis=0).astype(jnp.bfloat16)
        wide = jnp.dot(projectors[site], spread, preferred_element_type=jnp.float32)
        wide = fold_lanes(wide)
        packed = wide[:16]
        for p in range(1, per):
            packed = jnp.where(pack_lane == p, wide[16 * p : 16 * (p + 1)], packed)
        factors[site] = packed.astype(jnp.bfloat16)
        return carry

    lax.fori_loop(0, sites, factor, 0)

    def gate_remote(other, slot):
        return pltpu.make_async_remote_copy(
            src_ref=gate_outbox.at[other],
            dst_ref=gate_arrived.at[slot],
            send_sem=gate_send_sem.at[other],
            recv_sem=gate_recv_sem.at[slot],
            device_id=(other, core),
            device_id_type=MESH,
        )

    def gate_send(step, carry):
        other = lax.rem(me + step, regions)
        gate_outbox[other] = factors[gate_index[other]]
        gate_remote(other, me).start()
        return carry

    lax.fori_loop(1, regions, gate_send, 0)
    gate_arrived[me] = jnp.zeros_like(gate_arrived[me])

    def gate_collect(step, carry):
        other = lax.rem(me + step, regions)
        gate_remote(other, me).wait_send()
        gate_remote(other, other).wait_recv()
        return carry

    lax.fori_loop(1, regions, gate_collect, 0)
    factors[pl.ds(sites, regions)] = gate_arrived[...]
    factors[sites + regions] = jnp.zeros_like(factors[0])

    def gate_pick(site, carry):
        half[site] = factors[gate_src[site]]
        return carry

    lax.fori_loop(0, sites, gate_pick, 0)
    both[core] = half[...]
    swap = to_mate(half, both.at[core], SWEEPS)
    swap.start()
    swap.wait()

    def update_remote(site):
        return pltpu.make_async_remote_copy(
            src_ref=update_outbox.at[site],
            dst_ref=update_inbox.at[site],
            send_sem=update_send_sem.at[site],
            recv_sem=update_recv_sem.at[site],
            device_id=(me, 1 - core),
            device_id_type=MESH,
        )

    def mixed(site, new_spin):
        total = jnp.zeros((16, 128), jnp.float32)
        for spin in range(2):
            first = gate[(4 * new_spin + core) * 2 + spin]
            second = gate[(4 * new_spin + 2 + core) * 2 + spin]
            total = total + jnp.where(pack_lane < per // 2, first, second) * both[
                spin, site
            ].astype(jnp.float32)
        total = total + pltpu.roll(total, 64, 1)
        matrix = jnp.concatenate([total[:, :bond], total[:, bond : 2 * bond]], axis=0)
        return diagonal(matrix)

    def multiply(site, carry):
        factor_pair = jnp.concatenate([mixed(site, 1 - core), mixed(site, core)], axis=0)
        product = contract(split(chunks(tensors[site])), split(factor_pair), ((1,), (1,)))
        for j in range(pieces):
            part = product[bond * j : bond * (j + 1)]
            update_outbox[site, :, 128 * j : 128 * (j + 1)] = part[:, :128].astype(jnp.bfloat16)
            own[site, :, 128 * j : 128 * (j + 1)] = part[:, 128:]
        update_remote(site).start()
        return carry

    lax.fori_loop(0, sites, multiply, 0)

    def gather(site, carry):
        update_remote(site).wait()
        total = own[site] + update_inbox[site].astype(jnp.float32)
        own[site] = total
        squares[site] = jnp.sum((total * total).reshape(bond // 8, 8, width), axis=0)
        return carry

    lax.fori_loop(0, sites, gather, 0)
    summed = jnp.sum(squares[...], axis=(1, 2), keepdims=True)
    norms[0] = jnp.broadcast_to(summed, (sites, 8, 128))
    swap = to_mate(norms.at[0], norms.at[1], SWEEPS + 1)
    swap.start()
    swap.wait()

    def finish(site, carry):
        mean = (norms[0, site] + norms[1, site])[0:1, 0:1] / (2 * bond**3)
        updated = own[site] * lax.rsqrt(mean + EPSILON)
        new_out[site] = jnp.where(gate_src[site] == sites + regions, tensors[site], updated)
        return carry

    lax.fori_loop(0, sites, finish, 0)


def whole(regions, send_index, recv_src, gate_index, gate_src, gate, tensors, projectors, edge):
    sites, bond, width = tensors.shape
    messages = 3 * sites
    dma = pltpu.SemaphoreType.DMA
    return pl.pallas_call(
        functools.partial(whole_kernel, regions),
        out_shape=(
            jax.ShapeDtypeStruct(tensors.shape, jnp.float32),
            jax.ShapeDtypeStruct((sites, 3, width), jnp.float32),
        ),
        in_specs=[SMEM] * 5 + [VMEM] * 3,
        out_specs=(VMEM, VMEM),
        scratch_shapes=[
            pltpu.VMEM((messages, bond, 128), jnp.float32),
            pltpu.VMEM((6, bond * width // 128, 128), jnp.float32),
            pltpu.VMEM((3, bond, 128), jnp.float32),
            pltpu.VMEM((SWEEPS, messages, 8, 128), jnp.float32),
            pltpu.VMEM((SWEEPS, messages, 8, 128), jnp.float32),
            pltpu.VMEM((messages + regions * CAP + 1, 8, 128), jnp.float32),
            pltpu.VMEM((SWEEPS, regions, CAP, 8, 128), jnp.float32),
            pltpu.VMEM((SWEEPS, regions, CAP, 8, 128), jnp.float32),
            pltpu.VMEM((sites + regions + 1, 16, 128), jnp.bfloat16),
            pltpu.VMEM((regions, 16, 128), jnp.bfloat16),
            pltpu.VMEM((regions, 16, 128), jnp.bfloat16),
            pltpu.VMEM((2, sites, 16, 128), jnp.bfloat16),
            pltpu.VMEM((sites, 16, 128), jnp.bfloat16),
            pltpu.VMEM(tensors.shape, jnp.float32),
            pltpu.VMEM(tensors.shape, jnp.bfloat16),
            pltpu.VMEM(tensors.shape, jnp.bfloat16),
            pltpu.VMEM((sites, 8, width), jnp.float32),
            pltpu.VMEM((2, sites, 8, 128), jnp.float32),
            dma((2 * SWEEPS + 4,)),
            dma((SWEEPS, regions)),
            dma((SWEEPS, regions)),
            dma((regions,)),
            dma((regions,)),
            dma((sites,)),
            dma((sites,)),
        ],
        compiler_params=pltpu.CompilerParams(
            collective_id=0, has_side_effects=True, vmem_limit_bytes=48 * 2**20
        ),
    )(send_index, recv_src, gate_index, gate_src, gate, tensors, projectors, edge)


def shards(
    site_tensors,
    projectors,
    gate_matrix,
    recv_src,
    cut_list,
    cut_dest,
    gate_src,
    gate_list,
    gate_dest,
):
    site_count = site_tensors.shape[0]
    bond_dim = site_tensors.shape[2]
    regions = lax.axis_size("region")
    my_region = lax.axis_index("region")
    edge = jnp.zeros((bond_dim * bond_dim,), jnp.float32).at[0].set(bond_dim).reshape(8, 128)
    own_dest = lax.dynamic_index_in_dim(cut_dest, my_region, 0, keepdims=False)
    own_gate = lax.dynamic_index_in_dim(gate_dest, my_region, 0, keepdims=False)
    send_index = slots(cut_list, own_dest, regions * CAP)
    gate_index = slots(gate_list, own_gate, regions * GCAP)
    new_sites, messages = whole(
        regions,
        send_index,
        recv_src.reshape(-1),
        gate_index,
        gate_src,
        gate_matrix.reshape(-1),
        site_tensors.reshape(site_count, bond_dim, -1),
        projectors.reshape(site_count, 2 * bond_dim, -1),
        edge,
    )
    return (new_sites.reshape(site_tensors.shape), messages)


def solution(mesh):
    return jax.shard_map(
        shards,
        mesh=mesh,
        in_specs=(
            P("region", "blk", None, None),
            P("region", None, None, None),
            P(),
            P("region", None),
            P("region"),
            P(),
            P("region"),
            P("region"),
            P(),
        ),
        out_specs=(P("region", "blk", None, None), P("region", None, None)),
        check_vma=False,
    )
```

```python
import functools

import jax
import jax.numpy as jnp
from jax import lax
from jax.experimental import pallas as pl
from jax.experimental.pallas import tpu as pltpu
from jax.sharding import PartitionSpec as P

SWEEPS = 2
CAP = 4
GCAP = 1
EPSILON = 1e-06
VMEM = pl.BlockSpec(memory_space=pltpu.VMEM)
HBM = pl.BlockSpec(memory_space=pltpu.HBM)
SMEM = pl.BlockSpec(memory_space=pltpu.SMEM)
MESH = pl.DeviceIdType.MESH


def split(value):
    high = value.astype(jnp.bfloat16)
    low = (value - high.astype(jnp.float32)).astype(jnp.bfloat16)
    return high, low


def contract(left, right, dims):
    dot = functools.partial(
        lax.dot_general,
        dimension_numbers=(dims, ((), ())),
        preferred_element_type=jnp.float32,
    )
    return dot(left[0], right[0]) + (dot(left[1], right[0]) + dot(left[0], right[1]))


def chunks(rows):
    return jnp.concatenate(
        [rows[:, 128 * j : 128 * (j + 1)] for j in range(rows.shape[1] // 128)], axis=0
    )


def unchunk(stacked, bond):
    return jnp.concatenate(
        [stacked[bond * j : bond * (j + 1)] for j in range(stacked.shape[0] // bond)], axis=1
    )


def swap_axes(stacked, source, target, bond):
    per = 128 // bond
    groups = bond // per
    source[...] = stacked
    lane = lax.broadcasted_iota(jnp.int32, (groups * groups, 128), 1) // bond
    taken = [
        jnp.concatenate(
            [source[pl.ds(per * k + q, groups, stride=bond), :] for k in range(groups)], axis=0
        )
        for q in range(per)
    ]
    for p in range(per):
        merged = taken[p]
        for q in range(per):
            if q != p:
                moved = pltpu.roll(taken[q], (bond * (q - p)) % 128, 1)
                merged = jnp.where(lane == q, moved, merged)
        for k in range(groups):
            target[pl.ds(bond * k + p, groups, stride=per), :] = merged[
                groups * k : groups * (k + 1)
            ]
    return target[...]


def diagonal(matrix):
    bond = matrix.shape[0]
    per = 128 // bond
    wide = jnp.concatenate([matrix] * per, axis=1)
    tall = jnp.concatenate([wide] * per, axis=0)
    row = lax.broadcasted_iota(jnp.int32, (128, 128), 0) // bond
    column = lax.broadcasted_iota(jnp.int32, (128, 128), 1) // bond
    return jnp.where(row == column, tall, 0.0)


def slots(entries, dest_row, count):
    matched = dest_row[None, :] == jnp.arange(count, dtype=jnp.int32)[:, None]
    return jnp.sum(jnp.where(matched, entries[None, :], 0), axis=1).astype(jnp.int32)


def site_terms(tensors, current, site, swaps):
    bond = tensors.shape[1]
    rows, inner, outer = ((1,), (0,)), ((1,), (1,)), ((0,), (0,))
    wide = tensors[site]
    plain = chunks(wide)
    swapped = swap_axes(plain, swaps.at[0], swaps.at[1], bond)
    left = split(current[3 * site][:, :bond])
    right = split(current[3 * site + 1][:, :bond])
    vertical = split(diagonal(current[3 * site + 2][:, :bond]))
    on_a = contract(left, split(wide), outer)
    on_b = contract(right, split(unchunk(swapped, bond)), outer)
    on_a_stacked = chunks(on_a)
    on_a_swapped = unchunk(swap_axes(on_a_stacked, swaps.at[2], swaps.at[3], bond), bond)
    on_b_stacked = swap_axes(chunks(on_b), swaps.at[4], swaps.at[5], bond)
    on_b_swapped = unchunk(on_b_stacked, bond)
    on_c = unchunk(contract(split(plain), vertical, rows), bond)
    on_c_swapped = unchunk(contract(split(swapped), vertical, rows), bond)
    leg_zero = contract(split(on_b_swapped), split(on_c), inner)
    leg_one = contract(split(on_a_swapped), split(on_c_swapped), inner)
    crossed = contract(split(on_a_stacked), split(on_b_stacked), outer)
    crossed = jnp.where(same_block(bond), crossed, 0.0)
    folded = sum(crossed[bond * p : bond * (p + 1)] for p in range(128 // bond))
    return leg_zero, leg_one, fold_lanes(folded)[:, :bond]


def first_terms(tensors, opens, site, swaps):
    bond, width = tensors.shape[1:]
    inner, outer = ((1,), (1,)), ((0,), (0,))
    wide = tensors[site]
    plain = chunks(wide)
    swapped = unchunk(swap_axes(plain, swaps.at[0], swaps.at[1], bond), bond)
    row = lax.broadcasted_iota(jnp.int32, wide.shape, 0)
    lane = lax.broadcasted_iota(jnp.int32, wide.shape, 1)

    def scaled(value, index, leg):
        edge = jnp.where(index == 0, float(bond) * value, 0.0)
        return jnp.where(opens[leg], edge, value)

    on_a = split(chunks(scaled(wide, row, 0)))
    on_b_wide = scaled(wide, lane // bond, 1)
    on_b = split(chunks(on_b_wide))
    on_c = split(scaled(wide, lane % bond, 2))
    leg_zero = contract(split(on_b_wide), on_c, inner)
    on_a_swapped = split(scaled(swapped, lane // bond, 0))
    on_c_swapped = split(scaled(swapped, lane % bond, 2))
    leg_one = contract(on_a_swapped, on_c_swapped, inner)
    crossed = jnp.where(same_block(bond), contract(on_a, on_b, outer), 0.0)
    folded = sum(crossed[bond * p : bond * (p + 1)] for p in range(128 // bond))
    return leg_zero, leg_one, fold_lanes(folded)[:, :bond]


def same_block(bond):
    row = lax.broadcasted_iota(jnp.int32, (128, 128), 0) // bond
    column = lax.broadcasted_iota(jnp.int32, (128, 128), 1) // bond
    return row == column


def fold_lanes(value):
    value = value + pltpu.roll(value, 64, 1)
    return value + pltpu.roll(value, 32, 1)


def flatten(matrix, scratch):
    bond = matrix.shape[0]
    per = 128 // bond
    scratch[...] = jnp.concatenate([matrix] * per, axis=1)
    lane = lax.broadcasted_iota(jnp.int32, (bond // per, 128), 1) // bond
    flat = scratch[pl.ds(0, bond // per, stride=per), :]
    for p in range(1, per):
        flat = jnp.where(lane == p, scratch[pl.ds(p, bond // per, stride=per), :], flat)
    return flat


def whole_kernel(
    regions,
    table,
    gate,
    tensors_far,
    projectors_far,
    new_out,
    msg_out,
    tensors,
    projectors,
    first_outbox,
    first_arrived,
    current,
    swaps,
    flats,
    partial,
    mate,
    lookup,
    outbox,
    arrived,
    factors,
    gate_outbox,
    gate_arrived,
    both,
    half,
    own,
    update_outbox,
    update_inbox,
    squares,
    norms,
    mate_sem,
    send_sem,
    recv_sem,
    gate_send_sem,
    gate_recv_sem,
    update_send_sem,
    update_recv_sem,
    load_sem,
):
    me = lax.axis_index("region")
    core = lax.axis_index("blk")
    sites, bond, width = tensors.shape
    per = 128 // bond
    pieces = width // 128
    messages = 3 * sites
    none = messages + regions * CAP

    def send_index(entry):
        return table[entry]

    def gate_index(entry):
        return table[regions * CAP + entry]

    def recv_src(entry):
        return table[regions * (CAP + GCAP) + entry]

    def gate_src(entry):
        return table[regions * (CAP + GCAP) + messages + entry]

    def load(site):
        return pltpu.make_async_copy(tensors_far.at[site], tensors.at[site], load_sem.at[site])

    load_projectors = pltpu.make_async_copy(projectors_far, projectors, load_sem.at[sites])
    for site in range(sites):
        load(site).start()
    load_projectors.start()
    barrier = pltpu.get_barrier_semaphore()
    pl.semaphore_signal(barrier, inc=1, device_id=(me, 1 - core), device_id_type=MESH)

    def hello(step, carry):
        other = lax.rem(me + step, regions)
        pl.semaphore_signal(barrier, inc=1, device_id=(other, core), device_id_type=MESH)
        return carry

    lax.fori_loop(1, regions, hello, 0)

    def to_mate(source, target, index):
        return pltpu.make_async_remote_copy(
            src_ref=source,
            dst_ref=target,
            send_sem=mate_sem.at[2 * index],
            recv_sem=mate_sem.at[2 * index + 1],
            device_id=(me, 1 - core),
            device_id_type=MESH,
        )

    def unflatten(flat, entry):
        for p in range(per):
            moved = flat if p == 0 else pltpu.roll(flat, 128 - bond * p, 1)
            current[entry, pl.ds(p, bond // per, stride=per), :] = moved

    row = lax.broadcasted_iota(jnp.int32, (8, 128), 0)
    column = lax.broadcasted_iota(jnp.int32, (8, 128), 1)
    place = 128 * row + column
    diagonal_flat = (place // bond) == (place % bond)
    edge = jnp.where(place == 0, float(bond), 0.0)

    for sweep in range(SWEEPS):

        def terms(pair, carry, sweep=sweep):
            for lane in range(2):
                site = 2 * pair + lane
                if sweep == 0:
                    load(site).wait()
            for lane in range(2):
                site = 2 * pair + lane
                if sweep == 0:
                    opens = [recv_src(3 * site + leg) == none for leg in range(3)]
                    legs = first_terms(tensors, opens, site, swaps.at[lane])
                else:
                    legs = site_terms(tensors, current, site, swaps.at[lane])
                for leg in range(3):
                    partial[sweep, 3 * site + leg] = flatten(legs[leg], flats.at[lane, leg])
            return carry

        lax.fori_loop(0, sites // 2, terms, 0)
        if sweep == 0:
            pl.semaphore_wait(barrier, regions)
        swap = to_mate(partial.at[sweep], mate.at[sweep], sweep)
        swap.start()
        swap.wait()
        total = partial[sweep] + mate[sweep]
        trace = jnp.sum(jnp.where(diagonal_flat[None], total, 0.0), axis=(1, 2), keepdims=True)
        lookup[pl.ds(0, messages)] = bond * total / trace

        def remote(other, slot, sweep=sweep):
            return pltpu.make_async_remote_copy(
                src_ref=first_outbox.at[other] if sweep == 0 else outbox.at[other],
                dst_ref=first_arrived.at[slot] if sweep == 0 else arrived.at[slot],
                send_sem=send_sem.at[sweep, other],
                recv_sem=recv_sem.at[sweep, slot],
                device_id=(other, core),
                device_id_type=MESH,
            )

        def send(step, carry, sweep=sweep, remote=remote):
            other = lax.rem(me + step, regions)
            leaving = jnp.concatenate(
                [lookup[send_index(CAP * other + slot)] for slot in range(CAP)], axis=0
            )
            if sweep == 0:
                first_outbox[other] = leaving.astype(jnp.bfloat16)
            else:
                outbox[other] = leaving
            remote(other, me).start()
            return carry

        lax.fori_loop(1, regions, send, 0)
        landed = first_arrived if sweep == 0 else arrived
        landed[me] = jnp.zeros_like(landed[me])

        def collect(step, carry, remote=remote):
            other = lax.rem(me + step, regions)
            remote(other, me).wait_send()
            remote(other, other).wait_recv()
            return carry

        lax.fori_loop(1, regions, collect, 0)
        lookup[pl.ds(messages, regions * CAP)] = (
            landed[...].astype(jnp.float32).reshape(regions * CAP, 8, 128)
        )
        lookup[none] = edge

        def pick(site, carry, sweep=sweep):
            for leg in range(3):
                flat = lookup[recv_src(3 * site + leg)]
                unflatten(flat, 3 * site + leg)
                if sweep == SWEEPS - 1:
                    for j in range(pieces):
                        msg_out[site, leg : leg + 1, 128 * j : 128 * (j + 1)] = flat[j : j + 1]
            return carry

        lax.fori_loop(0, sites, pick, 0)

    outer = ((0,), (0,))
    same = same_block(bond)
    pack_lane = lax.broadcasted_iota(jnp.int32, (16, 128), 1) // bond

    load_projectors.wait()

    def factor(site, scratch):
        left = split(current[3 * site][:, :bond])
        right = split(current[3 * site + 1][:, :bond])
        on_a = contract(left, split(tensors[site]), outer)
        swapped = unchunk(swap_axes(chunks(on_a), scratch.at[0], scratch.at[1], bond), bond)
        weights = contract(right, split(swapped), outer)
        weights = weights.astype(jnp.bfloat16).astype(jnp.float32)
        tiles = [
            jnp.where(same, jnp.concatenate([weights[:, 128 * j : 128 * (j + 1)]] * per, axis=0), 0.0)
            for j in range(pieces)
        ]
        spread = jnp.concatenate(tiles, axis=0).astype(jnp.bfloat16)
        wide = jnp.dot(projectors[site], spread, preferred_element_type=jnp.float32)
        wide = fold_lanes(wide)
        packed = wide[:16]
        for p in range(1, per):
            packed = jnp.where(pack_lane == p, wide[16 * p : 16 * (p + 1)], packed)
        factors[site] = packed.astype(jnp.bfloat16)

    def factor_pair(pair, carry):
        for lane in range(2):
            factor(2 * pair + lane, swaps.at[lane])
        return carry

    lax.fori_loop(0, sites // 2, factor_pair, 0)

    def gate_remote(other, slot):
        return pltpu.make_async_remote_copy(
            src_ref=gate_outbox.at[other],
            dst_ref=gate_arrived.at[slot],
            send_sem=gate_send_sem.at[other],
            recv_sem=gate_recv_sem.at[slot],
            device_id=(other, core),
            device_id_type=MESH,
        )

    def gate_send(step, carry):
        other = lax.rem(me + step, regions)
        gate_outbox[other] = factors[gate_index(other)]
        gate_remote(other, me).start()
        return carry

    lax.fori_loop(1, regions, gate_send, 0)
    gate_arrived[me] = jnp.zeros_like(gate_arrived[me])

    def gate_collect(step, carry):
        other = lax.rem(me + step, regions)
        gate_remote(other, me).wait_send()
        gate_remote(other, other).wait_recv()
        return carry

    lax.fori_loop(1, regions, gate_collect, 0)
    factors[pl.ds(sites, regions)] = gate_arrived[...]
    factors[sites + regions] = jnp.zeros_like(factors[0])

    def gate_pick(site, carry):
        half[site] = factors[gate_src(site)]
        return carry

    lax.fori_loop(0, sites, gate_pick, 0)
    both[core] = half[...]
    swap = to_mate(half, both.at[core], SWEEPS)
    swap.start()
    swap.wait()

    def update_remote(site):
        return pltpu.make_async_remote_copy(
            src_ref=update_outbox.at[site],
            dst_ref=update_inbox.at[site],
            send_sem=update_send_sem.at[site],
            recv_sem=update_recv_sem.at[site],
            device_id=(me, 1 - core),
            device_id_type=MESH,
        )

    def mixed(site, new_spin):
        total = jnp.zeros((16, 128), jnp.float32)
        for spin in range(2):
            first = gate[(4 * new_spin + core) * 2 + spin]
            second = gate[(4 * new_spin + 2 + core) * 2 + spin]
            total = total + jnp.where(pack_lane < per // 2, first, second) * both[
                spin, site
            ].astype(jnp.float32)
        total = total + pltpu.roll(total, 64, 1)
        matrix = jnp.concatenate([total[:, :bond], total[:, bond : 2 * bond]], axis=0)
        return diagonal(matrix)

    def multiply(site, carry):
        factor_pair = jnp.concatenate([mixed(site, 1 - core), mixed(site, core)], axis=0)
        product = contract(split(chunks(tensors[site])), split(factor_pair), ((1,), (1,)))
        for j in range(pieces):
            part = product[bond * j : bond * (j + 1)]
            update_outbox[site, :, 128 * j : 128 * (j + 1)] = part[:, :128].astype(jnp.bfloat16)
            own[site, :, 128 * j : 128 * (j + 1)] = part[:, 128:]
        update_remote(site).start()
        return carry

    lax.fori_loop(0, sites, multiply, 0)

    def gather(site, carry):
        update_remote(site).wait()
        total = own[site] + update_inbox[site].astype(jnp.float32)
        own[site] = total
        squares[site] = jnp.sum((total * total).reshape(bond // 8, 8, width), axis=0)
        return carry

    lax.fori_loop(0, sites, gather, 0)
    summed = jnp.sum(squares[...], axis=(1, 2), keepdims=True)
    norms[0] = jnp.broadcast_to(summed, (sites, 8, 128))
    swap = to_mate(norms.at[0], norms.at[1], SWEEPS + 1)
    swap.start()
    swap.wait()

    def finish(site, carry):
        mean = (norms[0, site] + norms[1, site])[0:1, 0:1] / (2 * bond**3)
        updated = own[site] * lax.rsqrt(mean + EPSILON)
        new_out[site] = jnp.where(gate_src(site) == sites + regions, tensors[site], updated)
        return carry

    lax.fori_loop(0, sites, finish, 0)


def whole(regions, table, gate, tensors, projectors):
    sites, bond, width = tensors.shape
    messages = 3 * sites
    dma = pltpu.SemaphoreType.DMA
    return pl.pallas_call(
        functools.partial(whole_kernel, regions),
        out_shape=(
            jax.ShapeDtypeStruct(tensors.shape, jnp.float32),
            jax.ShapeDtypeStruct((sites, 3, width), jnp.float32),
        ),
        in_specs=[SMEM] * 2 + [HBM] * 2,
        out_specs=(VMEM, VMEM),
        scratch_shapes=[
            pltpu.VMEM(tensors.shape, jnp.float32),
            pltpu.VMEM(projectors.shape, jnp.bfloat16),
            pltpu.VMEM((regions, CAP * 8, 128), jnp.bfloat16),
            pltpu.VMEM((regions, CAP * 8, 128), jnp.bfloat16),
            pltpu.VMEM((messages, bond, 128), jnp.float32),
            pltpu.VMEM((2, 6, bond * width // 128, 128), jnp.float32),
            pltpu.VMEM((2, 3, bond, 128), jnp.float32),
            pltpu.VMEM((SWEEPS, messages, 8, 128), jnp.float32),
            pltpu.VMEM((SWEEPS, messages, 8, 128), jnp.float32),
            pltpu.VMEM((messages + regions * CAP + 1, 8, 128), jnp.float32),
            pltpu.VMEM((regions, CAP * 8, 128), jnp.float32),
            pltpu.VMEM((regions, CAP * 8, 128), jnp.float32),
            pltpu.VMEM((sites + regions + 1, 16, 128), jnp.bfloat16),
            pltpu.VMEM((regions, 16, 128), jnp.bfloat16),
            pltpu.VMEM((regions, 16, 128), jnp.bfloat16),
            pltpu.VMEM((2, sites, 16, 128), jnp.bfloat16),
            pltpu.VMEM((sites, 16, 128), jnp.bfloat16),
            pltpu.VMEM(tensors.shape, jnp.float32),
            pltpu.VMEM(tensors.shape, jnp.bfloat16),
            pltpu.VMEM(tensors.shape, jnp.bfloat16),
            pltpu.VMEM((sites, 8, width), jnp.float32),
            pltpu.VMEM((2, sites, 8, 128), jnp.float32),
            dma((2 * SWEEPS + 4,)),
            dma((SWEEPS, regions)),
            dma((SWEEPS, regions)),
            dma((regions,)),
            dma((regions,)),
            dma((sites,)),
            dma((sites,)),
            dma((sites + 1,)),
        ],
        compiler_params=pltpu.CompilerParams(
            collective_id=0, has_side_effects=True, vmem_limit_bytes=48 * 2**20
        ),
    )(table, gate, tensors, projectors)


def shards(
    site_tensors,
    projectors,
    gate_matrix,
    recv_src,
    cut_list,
    cut_dest,
    gate_src,
    gate_list,
    gate_dest,
):
    site_count = site_tensors.shape[0]
    bond_dim = site_tensors.shape[2]
    regions = lax.axis_size("region")
    my_region = lax.axis_index("region")
    own_dest = lax.dynamic_index_in_dim(cut_dest, my_region, 0, keepdims=False)
    own_gate = lax.dynamic_index_in_dim(gate_dest, my_region, 0, keepdims=False)
    send_index = slots(cut_list, own_dest, regions * CAP)
    gate_index = slots(gate_list, own_gate, regions * GCAP)
    table = jnp.concatenate([send_index, gate_index, recv_src.reshape(-1), gate_src])
    new_sites, messages = whole(
        regions,
        table,
        gate_matrix.reshape(-1),
        site_tensors.reshape(site_count, bond_dim, -1),
        projectors.reshape(site_count, 2 * bond_dim, -1),
    )
    return (new_sites.reshape(site_tensors.shape), messages)


def solution(mesh):
    return jax.shard_map(
        shards,
        mesh=mesh,
        in_specs=(
            P("region", "blk", None, None),
            P("region", None, None, None),
            P(),
            P("region", None),
            P("region"),
            P(),
            P("region"),
            P("region"),
            P(),
        ),
        out_specs=(P("region", "blk", None, None), P("region", None, None)),
        check_vma=False,
    )
```

```python
import functools

import jax
import jax.numpy as jnp
from jax import lax
from jax.experimental import pallas as pl
from jax.experimental.pallas import tpu as pltpu
from jax.sharding import PartitionSpec as P

SWEEPS = 2
CAP = 4
GCAP = 1
EPSILON = 1e-06
VMEM = pl.BlockSpec(memory_space=pltpu.VMEM)
HBM = pl.BlockSpec(memory_space=pltpu.HBM)
SMEM = pl.BlockSpec(memory_space=pltpu.SMEM)
MESH = pl.DeviceIdType.MESH


def split(value):
    high = value.astype(jnp.bfloat16)
    low = (value - high.astype(jnp.float32)).astype(jnp.bfloat16)
    return high, low


def contract(left, right, dims):
    dot = functools.partial(
        lax.dot_general,
        dimension_numbers=(dims, ((), ())),
        preferred_element_type=jnp.float32,
    )
    return dot(left[0], right[0]) + (dot(left[1], right[0]) + dot(left[0], right[1]))


def chunks(rows):
    return jnp.concatenate(
        [rows[:, 128 * j : 128 * (j + 1)] for j in range(rows.shape[1] // 128)], axis=0
    )


def unchunk(stacked, bond):
    return jnp.concatenate(
        [stacked[bond * j : bond * (j + 1)] for j in range(stacked.shape[0] // bond)], axis=1
    )


def swap_axes(stacked, source, target, bond):
    per = 128 // bond
    groups = bond // per
    source[...] = stacked
    lane = lax.broadcasted_iota(jnp.int32, (groups * groups, 128), 1) // bond
    taken = [
        jnp.concatenate(
            [source[pl.ds(per * k + q, groups, stride=bond), :] for k in range(groups)], axis=0
        )
        for q in range(per)
    ]
    for p in range(per):
        merged = taken[p]
        for q in range(per):
            if q != p:
                moved = pltpu.roll(taken[q], (bond * (q - p)) % 128, 1)
                merged = jnp.where(lane == q, moved, merged)
        for k in range(groups):
            target[pl.ds(bond * k + p, groups, stride=per), :] = merged[
                groups * k : groups * (k + 1)
            ]
    return target[...]


def diagonal(matrix):
    bond = matrix.shape[0]
    per = 128 // bond
    wide = jnp.concatenate([matrix] * per, axis=1)
    tall = jnp.concatenate([wide] * per, axis=0)
    row = lax.broadcasted_iota(jnp.int32, (128, 128), 0) // bond
    column = lax.broadcasted_iota(jnp.int32, (128, 128), 1) // bond
    return jnp.where(row == column, tall, 0.0)


def slots(entries, dest_row, count):
    matched = dest_row[None, :] == jnp.arange(count, dtype=jnp.int32)[:, None]
    return jnp.sum(jnp.where(matched, entries[None, :], 0), axis=1).astype(jnp.int32)


def site_terms(tensors, current, site, swaps):
    bond = tensors.shape[1]
    rows, inner, outer = ((1,), (0,)), ((1,), (1,)), ((0,), (0,))
    wide = tensors[site]
    plain = chunks(wide)
    swapped = swap_axes(plain, swaps.at[0], swaps.at[1], bond)
    left = split(current[3 * site][:, :bond])
    right = split(current[3 * site + 1][:, :bond])
    vertical = split(diagonal(current[3 * site + 2][:, :bond]))
    on_a = contract(left, split(wide), outer)
    on_b = contract(right, split(unchunk(swapped, bond)), outer)
    on_a_stacked = chunks(on_a)
    on_a_swapped = unchunk(swap_axes(on_a_stacked, swaps.at[2], swaps.at[3], bond), bond)
    on_b_stacked = swap_axes(chunks(on_b), swaps.at[4], swaps.at[5], bond)
    on_b_swapped = unchunk(on_b_stacked, bond)
    on_c = unchunk(contract(split(plain), vertical, rows), bond)
    on_c_swapped = unchunk(contract(split(swapped), vertical, rows), bond)
    leg_zero = contract(split(on_b_swapped), split(on_c), inner)
    leg_one = contract(split(on_a_swapped), split(on_c_swapped), inner)
    crossed = contract(split(on_a_stacked), split(on_b_stacked), outer)
    crossed = jnp.where(same_block(bond), crossed, 0.0)
    folded = sum(crossed[bond * p : bond * (p + 1)] for p in range(128 // bond))
    return leg_zero, leg_one, fold_lanes(folded)[:, :bond]


def first_terms(tensors, opens, site, swaps):
    bond, width = tensors.shape[1:]
    inner, outer = ((1,), (1,)), ((0,), (0,))
    wide = tensors[site]
    plain = chunks(wide)
    swapped = unchunk(swap_axes(plain, swaps.at[0], swaps.at[1], bond), bond)
    row = lax.broadcasted_iota(jnp.int32, wide.shape, 0)
    lane = lax.broadcasted_iota(jnp.int32, wide.shape, 1)

    def scaled(value, index, leg):
        edge = jnp.where(index == 0, float(bond) * value, 0.0)
        return jnp.where(opens[leg], edge, value)

    on_a = split(chunks(scaled(wide, row, 0)))
    on_b_wide = scaled(wide, lane // bond, 1)
    on_b = split(chunks(on_b_wide))
    on_c = split(scaled(wide, lane % bond, 2))
    leg_zero = contract(split(on_b_wide), on_c, inner)
    on_a_swapped = split(scaled(swapped, lane // bond, 0))
    on_c_swapped = split(scaled(swapped, lane % bond, 2))
    leg_one = contract(on_a_swapped, on_c_swapped, inner)
    crossed = jnp.where(same_block(bond), contract(on_a, on_b, outer), 0.0)
    folded = sum(crossed[bond * p : bond * (p + 1)] for p in range(128 // bond))
    return leg_zero, leg_one, fold_lanes(folded)[:, :bond]


def same_block(bond):
    row = lax.broadcasted_iota(jnp.int32, (128, 128), 0) // bond
    column = lax.broadcasted_iota(jnp.int32, (128, 128), 1) // bond
    return row == column


def fold_lanes(value):
    value = value + pltpu.roll(value, 64, 1)
    return value + pltpu.roll(value, 32, 1)


def flatten(matrix, scratch):
    bond = matrix.shape[0]
    per = 128 // bond
    scratch[...] = jnp.concatenate([matrix] * per, axis=1)
    lane = lax.broadcasted_iota(jnp.int32, (bond // per, 128), 1) // bond
    flat = scratch[pl.ds(0, bond // per, stride=per), :]
    for p in range(1, per):
        flat = jnp.where(lane == p, scratch[pl.ds(p, bond // per, stride=per), :], flat)
    return flat


def whole_kernel(
    regions,
    table,
    gate,
    tensors_far,
    projectors_far,
    new_out,
    msg_out,
    tensors,
    projectors,
    first_outbox,
    first_arrived,
    current,
    swaps,
    flats,
    partial,
    mate,
    lookup,
    outbox,
    arrived,
    factors,
    gate_outbox,
    gate_arrived,
    both,
    half,
    own,
    update_outbox,
    update_inbox,
    squares,
    norms,
    mate_sem,
    send_sem,
    recv_sem,
    gate_send_sem,
    gate_recv_sem,
    update_send_sem,
    update_recv_sem,
    load_sem,
):
    me = lax.axis_index("region")
    core = lax.axis_index("blk")
    sites, bond, width = tensors.shape
    per = 128 // bond
    pieces = width // 128
    messages = 3 * sites
    none = messages + regions * CAP

    def send_index(entry):
        return table[entry]

    def gate_index(entry):
        return table[regions * CAP + entry]

    def recv_src(entry):
        return table[regions * (CAP + GCAP) + entry]

    def gate_src(entry):
        return table[regions * (CAP + GCAP) + messages + entry]

    def load(site):
        return pltpu.make_async_copy(tensors_far.at[site], tensors.at[site], load_sem.at[site])

    load_projectors = pltpu.make_async_copy(projectors_far, projectors, load_sem.at[sites])
    for site in range(sites):
        load(site).start()
    load_projectors.start()
    barrier = pltpu.get_barrier_semaphore()
    pl.semaphore_signal(barrier, inc=1, device_id=(me, 1 - core), device_id_type=MESH)

    def hello(step, carry):
        other = lax.rem(me + step, regions)
        pl.semaphore_signal(barrier, inc=1, device_id=(other, core), device_id_type=MESH)
        return carry

    lax.fori_loop(1, regions, hello, 0)

    def to_mate(source, target, index):
        return pltpu.make_async_remote_copy(
            src_ref=source,
            dst_ref=target,
            send_sem=mate_sem.at[2 * index],
            recv_sem=mate_sem.at[2 * index + 1],
            device_id=(me, 1 - core),
            device_id_type=MESH,
        )

    def unflatten(flat, entry):
        for p in range(per):
            moved = flat if p == 0 else pltpu.roll(flat, 128 - bond * p, 1)
            current[entry, pl.ds(p, bond // per, stride=per), :] = moved

    row = lax.broadcasted_iota(jnp.int32, (8, 128), 0)
    column = lax.broadcasted_iota(jnp.int32, (8, 128), 1)
    place = 128 * row + column
    diagonal_flat = (place // bond) == (place % bond)
    edge = jnp.where(place == 0, float(bond), 0.0)

    for sweep in range(SWEEPS):

        def terms(pair, carry, sweep=sweep):
            for lane in range(2):
                site = 2 * pair + lane
                if sweep == 0:
                    load(site).wait()
            for lane in range(2):
                site = 2 * pair + lane
                if sweep == 0:
                    opens = [recv_src(3 * site + leg) == none for leg in range(3)]
                    legs = first_terms(tensors, opens, site, swaps.at[lane])
                else:
                    legs = site_terms(tensors, current, site, swaps.at[lane])
                for leg in range(3):
                    partial[sweep, 3 * site + leg] = flatten(legs[leg], flats.at[lane, leg])
            return carry

        lax.fori_loop(0, sites // 2, terms, 0)
        if sweep == 0:
            pl.semaphore_wait(barrier, regions)
        swap = to_mate(partial.at[sweep], mate.at[sweep], sweep)
        swap.start()
        swap.wait()
        total = partial[sweep] + mate[sweep]
        trace = jnp.sum(jnp.where(diagonal_flat[None], total, 0.0), axis=(1, 2), keepdims=True)
        lookup[pl.ds(0, messages)] = bond * total / trace

        def remote(other, slot, sweep=sweep):
            return pltpu.make_async_remote_copy(
                src_ref=first_outbox.at[other] if sweep == 0 else outbox.at[other],
                dst_ref=first_arrived.at[slot] if sweep == 0 else arrived.at[slot],
                send_sem=send_sem.at[sweep, other],
                recv_sem=recv_sem.at[sweep, slot],
                device_id=(other, core),
                device_id_type=MESH,
            )

        def send(step, carry, sweep=sweep, remote=remote):
            other = lax.rem(me + step, regions)
            leaving = jnp.concatenate(
                [lookup[send_index(CAP * other + slot)] for slot in range(CAP)], axis=0
            )
            if sweep == 0:
                first_outbox[other] = leaving.astype(jnp.bfloat16)
            else:
                outbox[other] = leaving
            remote(other, me).start()
            return carry

        lax.fori_loop(1, regions, send, 0)
        landed = first_arrived if sweep == 0 else arrived
        landed[me] = jnp.zeros_like(landed[me])

        def collect(step, carry, remote=remote):
            other = lax.rem(me + step, regions)
            remote(other, me).wait_send()
            remote(other, other).wait_recv()
            return carry

        lax.fori_loop(1, regions, collect, 0)
        lookup[pl.ds(messages, regions * CAP)] = (
            landed[...].astype(jnp.float32).reshape(regions * CAP, 8, 128)
        )
        lookup[none] = edge

        def pick(site, carry, sweep=sweep):
            for leg in range(3):
                flat = lookup[recv_src(3 * site + leg)]
                unflatten(flat, 3 * site + leg)
                if sweep == SWEEPS - 1:
                    for j in range(pieces):
                        msg_out[site, leg : leg + 1, 128 * j : 128 * (j + 1)] = flat[j : j + 1]
            return carry

        lax.fori_loop(0, sites, pick, 0)

    outer = ((0,), (0,))
    same = same_block(bond)
    pack_lane = lax.broadcasted_iota(jnp.int32, (16, 128), 1) // bond

    load_projectors.wait()

    def factor(site, scratch):
        left = split(current[3 * site][:, :bond])
        right = split(current[3 * site + 1][:, :bond])
        on_a = contract(left, split(tensors[site]), outer)
        swapped = unchunk(swap_axes(chunks(on_a), scratch.at[0], scratch.at[1], bond), bond)
        weights = contract(right, split(swapped), outer)
        weights = weights.astype(jnp.bfloat16).astype(jnp.float32)
        tiles = [
            jnp.where(same, jnp.concatenate([weights[:, 128 * j : 128 * (j + 1)]] * per, axis=0), 0.0)
            for j in range(pieces)
        ]
        spread = jnp.concatenate(tiles, axis=0).astype(jnp.bfloat16)
        wide = jnp.dot(projectors[site], spread, preferred_element_type=jnp.float32)
        wide = fold_lanes(wide)
        packed = wide[:16]
        for p in range(1, per):
            packed = jnp.where(pack_lane == p, wide[16 * p : 16 * (p + 1)], packed)
        factors[site] = packed.astype(jnp.bfloat16)

    def factor_pair(pair, carry):
        for lane in range(2):
            factor(2 * pair + lane, swaps.at[lane])
        return carry

    lax.fori_loop(0, sites // 2, factor_pair, 0)

    def gate_remote(other, slot):
        return pltpu.make_async_remote_copy(
            src_ref=gate_outbox.at[other],
            dst_ref=gate_arrived.at[slot],
            send_sem=gate_send_sem.at[other],
            recv_sem=gate_recv_sem.at[slot],
            device_id=(other, core),
            device_id_type=MESH,
        )

    def gate_send(step, carry):
        other = lax.rem(me + step, regions)
        gate_outbox[other] = factors[gate_index(other)]
        gate_remote(other, me).start()
        return carry

    lax.fori_loop(1, regions, gate_send, 0)
    gate_arrived[me] = jnp.zeros_like(gate_arrived[me])

    def gate_collect(step, carry):
        other = lax.rem(me + step, regions)
        gate_remote(other, me).wait_send()
        gate_remote(other, other).wait_recv()
        return carry

    lax.fori_loop(1, regions, gate_collect, 0)
    factors[pl.ds(sites, regions)] = gate_arrived[...]
    factors[sites + regions] = jnp.zeros_like(factors[0])

    def gate_pick(site, carry):
        half[site] = factors[gate_src(site)]
        return carry

    lax.fori_loop(0, sites, gate_pick, 0)
    both[core] = half[...]
    swap = to_mate(half, both.at[core], SWEEPS)
    swap.start()
    swap.wait()

    def update_remote(site):
        return pltpu.make_async_remote_copy(
            src_ref=update_outbox.at[site],
            dst_ref=update_inbox.at[site],
            send_sem=update_send_sem.at[site],
            recv_sem=update_recv_sem.at[site],
            device_id=(me, 1 - core),
            device_id_type=MESH,
        )

    def mixed(site, new_spin):
        total = jnp.zeros((16, 128), jnp.float32)
        for spin in range(2):
            first = gate[(4 * new_spin + core) * 2 + spin]
            second = gate[(4 * new_spin + 2 + core) * 2 + spin]
            total = total + jnp.where(pack_lane < per // 2, first, second) * both[
                spin, site
            ].astype(jnp.float32)
        total = total + pltpu.roll(total, 64, 1)
        matrix = jnp.concatenate([total[:, :bond], total[:, bond : 2 * bond]], axis=0)
        return diagonal(matrix)

    def multiply(site):
        factor_pair = jnp.concatenate([mixed(site, 1 - core), mixed(site, core)], axis=0)
        product = contract(split(chunks(tensors[site])), split(factor_pair), ((1,), (1,)))
        for j in range(pieces):
            part = product[bond * j : bond * (j + 1)]
            update_outbox[site, :, 128 * j : 128 * (j + 1)] = part[:, :128].astype(jnp.bfloat16)
            own[site, :, 128 * j : 128 * (j + 1)] = part[:, 128:]
        update_remote(site).start()

    def multiply_pair(pair, carry):
        for lane in range(2):
            multiply(2 * pair + lane)
        return carry

    lax.fori_loop(0, sites // 2, multiply_pair, 0)

    def gather(site, carry):
        update_remote(site).wait()
        total = own[site] + update_inbox[site].astype(jnp.float32)
        own[site] = total
        squares[site] = jnp.sum((total * total).reshape(bond // 8, 8, width), axis=0)
        return carry

    lax.fori_loop(0, sites, gather, 0)
    summed = jnp.sum(squares[...], axis=(1, 2), keepdims=True)
    norms[0] = jnp.broadcast_to(summed, (sites, 8, 128))
    swap = to_mate(norms.at[0], norms.at[1], SWEEPS + 1)
    swap.start()
    swap.wait()

    def finish(site, carry):
        mean = (norms[0, site] + norms[1, site])[0:1, 0:1] / (2 * bond**3)
        updated = own[site] * lax.rsqrt(mean + EPSILON)
        new_out[site] = jnp.where(gate_src(site) == sites + regions, tensors[site], updated)
        return carry

    lax.fori_loop(0, sites, finish, 0)


def whole(regions, table, gate, tensors, projectors):
    sites, bond, width = tensors.shape
    messages = 3 * sites
    dma = pltpu.SemaphoreType.DMA
    return pl.pallas_call(
        functools.partial(whole_kernel, regions),
        out_shape=(
            jax.ShapeDtypeStruct(tensors.shape, jnp.float32),
            jax.ShapeDtypeStruct((sites, 3, width), jnp.float32),
        ),
        in_specs=[SMEM] * 2 + [HBM] * 2,
        out_specs=(VMEM, VMEM),
        scratch_shapes=[
            pltpu.VMEM(tensors.shape, jnp.float32),
            pltpu.VMEM(projectors.shape, jnp.bfloat16),
            pltpu.VMEM((regions, CAP * 8, 128), jnp.bfloat16),
            pltpu.VMEM((regions, CAP * 8, 128), jnp.bfloat16),
            pltpu.VMEM((messages, bond, 128), jnp.float32),
            pltpu.VMEM((2, 6, bond * width // 128, 128), jnp.float32),
            pltpu.VMEM((2, 3, bond, 128), jnp.float32),
            pltpu.VMEM((SWEEPS, messages, 8, 128), jnp.float32),
            pltpu.VMEM((SWEEPS, messages, 8, 128), jnp.float32),
            pltpu.VMEM((messages + regions * CAP + 1, 8, 128), jnp.float32),
            pltpu.VMEM((regions, CAP * 8, 128), jnp.float32),
            pltpu.VMEM((regions, CAP * 8, 128), jnp.float32),
            pltpu.VMEM((sites + regions + 1, 16, 128), jnp.bfloat16),
            pltpu.VMEM((regions, 16, 128), jnp.bfloat16),
            pltpu.VMEM((regions, 16, 128), jnp.bfloat16),
            pltpu.VMEM((2, sites, 16, 128), jnp.bfloat16),
            pltpu.VMEM((sites, 16, 128), jnp.bfloat16),
            pltpu.VMEM(tensors.shape, jnp.float32),
            pltpu.VMEM(tensors.shape, jnp.bfloat16),
            pltpu.VMEM(tensors.shape, jnp.bfloat16),
            pltpu.VMEM((sites, 8, width), jnp.float32),
            pltpu.VMEM((2, sites, 8, 128), jnp.float32),
            dma((2 * SWEEPS + 4,)),
            dma((SWEEPS, regions)),
            dma((SWEEPS, regions)),
            dma((regions,)),
            dma((regions,)),
            dma((sites,)),
            dma((sites,)),
            dma((sites + 1,)),
        ],
        compiler_params=pltpu.CompilerParams(
            collective_id=0, has_side_effects=True, vmem_limit_bytes=60 * 2**20
        ),
    )(table, gate, tensors, projectors)


def shards(
    site_tensors,
    projectors,
    gate_matrix,
    recv_src,
    cut_list,
    cut_dest,
    gate_src,
    gate_list,
    gate_dest,
):
    site_count = site_tensors.shape[0]
    bond_dim = site_tensors.shape[2]
    regions = lax.axis_size("region")
    my_region = lax.axis_index("region")
    own_dest = lax.dynamic_index_in_dim(cut_dest, my_region, 0, keepdims=False)
    own_gate = lax.dynamic_index_in_dim(gate_dest, my_region, 0, keepdims=False)
    send_index = slots(cut_list, own_dest, regions * CAP)
    gate_index = slots(gate_list, own_gate, regions * GCAP)
    table = jnp.concatenate([send_index, gate_index, recv_src.reshape(-1), gate_src])
    new_sites, messages = whole(
        regions,
        table,
        gate_matrix.reshape(-1),
        site_tensors.reshape(site_count, bond_dim, -1),
        projectors.reshape(site_count, 2 * bond_dim, -1),
    )
    return (new_sites.reshape(site_tensors.shape), messages)


def solution(mesh):
    return jax.shard_map(
        shards,
        mesh=mesh,
        in_specs=(
            P("region", "blk", None, None),
            P("region", None, None, None),
            P(),
            P("region", None),
            P("region"),
            P(),
            P("region"),
            P("region"),
            P(),
        ),
        out_specs=(P("region", "blk", None, None), P("region", None, None)),
        check_vma=False,
    )
```
